32 devices in a mesh: gx: 4 (over y, x), gy: 8 (over z, core).
Axes of the slice: x: 2, y: 2, z: 4, core: 2. Of those that a mesh axis runs over, the one named last changes fastest.
Arguments:
- velocity: bfloat16 [3, 64, 256, 256], P(None, 'gx', 'gy'), may hold values from -4 to 4
- density: bfloat16 [64, 256, 256], P('gx', 'gy'), may hold values from 0 to 1
Outputs:
- projected: float32 [3, 64, 256, 256], P(None, 'gx', 'gy')
- emission: float32 [64, 256, 256], P('gx', 'gy')
The draws below stay inside these ranges and needn't reach their ends.
All inputs are finite; a program needn't handle non-finite values.
Results may differ from the reference program's by a relative error of at most 0.0003.
Values sent between devices are 32-bit elements; how exact they have to be, the bound alone decides.
A program may use at most 64 MiB of HBM per device.

```python
import jax
import jax.numpy as jnp
from jax import lax

NZ = 256
NX = 64
NY = 256


def levels(rng, dims, pieces, low, top_value):
    def one(axis_at, blocks):
        steps = jax.random.uniform(jax.random.fold_in(jax.random.fold_in(rng, 6), axis_at), (blocks,), jnp.float32, low / len(pieces), top_value / len(pieces))
        return jnp.repeat(jnp.exp(steps), dims[axis_at] // blocks).reshape((-1,) + (1,) * (len(dims) - axis_at - 1))

    factor_of = one(*pieces[0])
    for cut in pieces[1:]:
        factor_of = factor_of * one(*cut)
    return factor_of


def scatter_about(stream_key, dims, deviation, reach, split=(), kind=jnp.bfloat16):
    entries = jax.random.normal(stream_key, dims, jnp.float32) * deviation
    if len(split) > 0:
        entries = levels(stream_key, dims, split, -0.22, 0.18) * entries
    return jnp.clip(entries, min=-reach, max=reach).astype(kind)


def setup_inputs(seed: int = 0) -> dict:
    splits = jax.random.split(jax.random.key(seed), 3)
    velocity = scatter_about(splits[0], (3, NX, NY, NZ), 1.0, 4.0, ((1, 4), (2, 8)))
    density = jnp.clip(1.0 * jax.random.uniform(splits[1], (NX, NY, NZ), jnp.float32) ** levels(splits[1], (NX, NY, NZ), ((0, 4), (1, 8)), -0.2, 0.2), 0.0, 1.0).astype(jnp.bfloat16)
    return {"velocity": velocity, "density": density}


time_step = 0.4
buoyancy = 2.0
extinction = 3.0
highest = lax.Precision.HIGHEST

def cosine_table(length):
    modes = jnp.arange(length, dtype=jnp.float32)[:, None]
    centres = jnp.arange(length, dtype=jnp.float32)[None, :] + 0.5
    factor = jnp.where(modes == 0, jnp.sqrt(1.0 / length), jnp.sqrt(2.0 / length))
    return (factor * jnp.cos(jnp.pi * modes * centres / length)).astype(jnp.float32)

def flux_terms(padded):
    extent = padded.shape

    def window(offset_x, offset_y, offset_z):
        return padded[:, 2 + offset_x:extent[1] - 2 + offset_x, 2 + offset_y:extent[2] - 2 + offset_y, 2 + offset_z:extent[3] - 2 + offset_z]

    def moved(axis_id, offset):
        offsets = [0, 0, 0]
        offsets[axis_id] = offset
        return window(offsets[0], offsets[1], offsets[2])
    middle = window(0, 0, 0)
    summed = jnp.zeros_like(middle)
    for axis_id in range(3):
        plus_one = moved(axis_id, 1)
        plus_two = moved(axis_id, 2)
        minus_one = moved(axis_id, -1)
        minus_two = moved(axis_id, -2)
        lower_diff = (2.0 * plus_one + 3.0 * middle - 6.0 * minus_one + minus_two) / 6.0
        upper_diff = (-plus_two + 6.0 * plus_one - 3.0 * middle - 2.0 * minus_one) / 6.0
        speed_axis = middle[axis_id]
        summed = summed + jnp.maximum(speed_axis, 0.0) * lower_diff + jnp.minimum(speed_axis, 0.0) * upper_diff
    return -summed

def close_walls(fields):
    open_x = (jnp.arange(NX) < NX - 1)[:, None, None]
    open_y = (jnp.arange(NY) < NY - 1)[None, :, None]
    open_z = (jnp.arange(NZ) < NZ - 1)[None, None, :]
    return jnp.stack([fields[0] * open_x, fields[1] * open_y, fields[2] * open_z, fields[3]])

def eigen_row(length):
    modes = jnp.arange(length, dtype=jnp.float32)
    return 2.0 - 2.0 * jnp.cos(jnp.pi * modes / length)

def reference(velocity, density):
    fields = jnp.concatenate([velocity.astype(jnp.float32), density.astype(jnp.float32)[None]], axis=0)
    margins = ((0, 0), (2, 2), (2, 2), (2, 2))
    section_one = close_walls(fields + time_step * flux_terms(jnp.pad(fields, margins)))
    section_two = close_walls(0.5 * fields + 0.5 * (section_one + time_step * flux_terms(jnp.pad(section_one, margins))))
    smoke_now = section_two[3]
    smoke_above = jnp.concatenate([smoke_now[:, :, 1:], jnp.zeros_like(smoke_now[:, :, :1])], axis=2)
    lifted = close_walls(jnp.stack([section_two[0], section_two[1], section_two[2] + time_step * buoyancy * 0.5 * (smoke_now + smoke_above), smoke_now]))
    below_x = jnp.concatenate([jnp.zeros_like(lifted[0][:1]), lifted[0][:-1]], axis=0)
    below_y = jnp.concatenate([jnp.zeros_like(lifted[1][:, :1]), lifted[1][:, :-1]], axis=1)
    below_z = jnp.concatenate([jnp.zeros_like(lifted[2][:, :, :1]), lifted[2][:, :, :-1]], axis=2)
    divergence = lifted[0] - below_x + (lifted[1] - below_y) + (lifted[2] - below_z)
    table_x = cosine_table(NX)
    table_y = cosine_table(NY)
    table_z = cosine_table(NZ)
    spectrum = jnp.einsum('xyn,kn->xyk', divergence, table_z, precision=highest)
    spectrum = jnp.einsum('xyk,ix->iyk', spectrum, table_x, precision=highest)
    spectrum = jnp.einsum('iyk,jy->ijk', spectrum, table_y, precision=highest)
    eigen_sum = eigen_row(NZ)[None, None, :] + eigen_row(NX)[:, None, None] + eigen_row(NY)[None, :, None]
    zero_mode = ((jnp.arange(NX) == 0)[:, None, None] & (jnp.arange(NY) == 0)[None, :, None] & (jnp.arange(NZ) == 0)[None, None, :]).astype(jnp.float32)
    pressure_hat = -spectrum * (1.0 - zero_mode) / (eigen_sum + zero_mode)
    pressure = jnp.einsum('ijk,ix->xjk', pressure_hat, table_x, precision=highest)
    pressure = jnp.einsum('xjk,jy->xyk', pressure, table_y, precision=highest)
    pressure = jnp.einsum('xyk,kn->xyn', pressure, table_z, precision=highest)
    grad_x = jnp.concatenate([pressure[1:], jnp.zeros_like(pressure[:1])], axis=0) - pressure
    grad_y = jnp.concatenate([pressure[:, 1:], jnp.zeros_like(pressure[:, :1])], axis=1) - pressure
    grad_z = jnp.concatenate([pressure[:, :, 1:], jnp.zeros_like(pressure[:, :, :1])], axis=2) - pressure
    projected = close_walls(jnp.stack([lifted[0] - grad_x, lifted[1] - grad_y, lifted[2] - grad_z, lifted[3]]))[:3]
    attenuation = extinction / NX
    optical = attenuation * (jnp.cumsum(smoke_now, axis=0) - smoke_now)
    emission = jnp.exp(-optical) * -jnp.expm1(-attenuation * smoke_now) / attenuation
    return (projected, emission)
```

```python
import functools

import jax
import jax.numpy as jnp
from jax import lax
from jax.experimental import pallas as pl
from jax.experimental.pallas import tpu as pltpu
from jax.sharding import PartitionSpec as P
import numpy as np

time_step = 0.4
buoyancy = 2.0
extinction = 3.0
highest = lax.Precision.HIGHEST


def padded_2(block, sides, width):
    for axis, dim in sides:
        count = lax.axis_size(axis)
        forward = [(i, i + 1) for i in range(count - 1)]
        backward = [(target, source) for source, target in forward]
        low = lax.ppermute(
            lax.slice_in_dim(block, block.shape[dim] - width, None, axis=dim), axis, forward
        )
        high = lax.ppermute(lax.slice_in_dim(block, 0, width, axis=dim), axis, backward)
        block = jnp.concatenate([low, block, high], axis=dim)
    return block


def cosine_table(length):
    modes = np.arange(length)[:, None]
    centres = np.arange(length)[None, :] + 0.5
    factor = np.where(modes == 0, np.sqrt(1.0 / length), np.sqrt(2.0 / length))
    return (factor * np.cos(np.pi * modes * centres / length)).astype(np.float32)


def flux_terms(padded):
    extent = padded.shape

    def window(offset_x, offset_y, offset_z):
        return padded[
            :,
            2 + offset_x : extent[1] - 2 + offset_x,
            2 + offset_y : extent[2] - 2 + offset_y,
            2 + offset_z : extent[3] - 2 + offset_z,
        ]

    def moved(axis_id, offset):
        offsets = [0, 0, 0]
        offsets[axis_id] = offset
        return window(offsets[0], offsets[1], offsets[2])

    middle = window(0, 0, 0)
    summed = jnp.zeros_like(middle)
    for axis_id in range(3):
        plus_one = moved(axis_id, 1)
        plus_two = moved(axis_id, 2)
        minus_one = moved(axis_id, -1)
        minus_two = moved(axis_id, -2)
        lower_diff = (2.0 * plus_one + 3.0 * middle - 6.0 * minus_one + minus_two) / 6.0
        upper_diff = (-plus_two + 6.0 * plus_one - 3.0 * middle - 2.0 * minus_one) / 6.0
        speed_axis = middle[axis_id]
        summed = (
            summed
            + jnp.maximum(speed_axis, 0.0) * lower_diff
            + jnp.minimum(speed_axis, 0.0) * upper_diff
        )
    return -summed


def tendency_rim(extended):
    return flux_terms(jnp.pad(extended, ((0, 0), (0, 0), (0, 0), (2, 2))))


def cropped(extended, have_rim, want_rim):
    cut_size = have_rim - want_rim
    return extended[
        :, cut_size : extended.shape[1] - cut_size, cut_size : extended.shape[2] - cut_size, :
    ]


def advect_halo(fields, rim_width):
    return padded_2(fields, (("gx", 1), ("gy", 2)), rim_width)


def halves(value):
    big = value.astype(jnp.bfloat16)
    return big, (value - big.astype(jnp.float32)).astype(jnp.bfloat16)


def dot_split(left, right):
    left_big, left_rest = halves(left)
    right_big, right_rest = halves(right)

    def dot(one, two):
        return jnp.dot(one, two, preferred_element_type=jnp.float32)

    return dot(left_big, right_big) + (dot(left_big, right_rest) + dot(left_rest, right_big))


def mode_tables(full_x, length_z, slab, groups, anchor_kz):
    modes_x = jnp.arange(full_x, dtype=jnp.float32)[:, None]
    modes_z = (anchor_kz + jnp.arange(slab * groups) % slab).astype(jnp.float32)[None, :]
    shift = 4.0 * (
        jnp.sin(modes_x * (np.pi / (2 * full_x))) ** 2
        + jnp.sin(modes_z * (np.pi / (2 * length_z))) ** 2
    )
    root = jnp.sqrt(shift + 0.25 * shift * shift)
    decay = 1.0 / (1.0 + 0.5 * shift + root)
    zero = (modes_x == 0) & (modes_z == 0)
    gain = jnp.where(zero, 0.0, -0.5 / jnp.where(zero, 1.0, root))
    return decay, gain


def solve_kernel(
    count_x,
    count_y,
    div_ref,
    lifted_ref,
    total_ref,
    tz_ref,
    tzt_ref,
    tx_ref,
    txt_ref,
    decay_ref,
    gain_ref,
    out_ref,
    before_ref,
    send_a,
    recv_a,
    send_b,
    recv_b,
    send_e,
    recv_e,
    edge,
    totals,
    sums,
    hat,
    sems_x,
    sems_y,
):
    block_x, block_y, length_z = div_ref.shape
    full_x = block_x * count_x
    me_x = lax.axis_index("gx")
    me_y = lax.axis_index("gy")
    slab = length_z // count_x
    lanes = recv_a.shape[-1]
    groups = lanes // slab
    rows = block_y // groups

    barrier = pltpu.get_barrier_semaphore()
    for offset in range(1, count_x):
        pl.semaphore_signal(
            barrier,
            inc=1,
            device_id={"gx": lax.rem(me_x + offset, count_x)},
            device_id_type=pl.DeviceIdType.MESH,
        )
    for offset in range(1, count_y):
        pl.semaphore_signal(
            barrier,
            inc=1,
            device_id={"gy": lax.rem(me_y + offset, count_y)},
            device_id_type=pl.DeviceIdType.MESH,
        )
    div = jnp.swapaxes(div_ref[...], 0, 1).reshape(block_y * block_x, length_z)
    along = dot_split(div, tzt_ref[...]).reshape(block_y, block_x, length_z)
    for target in range(count_x):
        send_a[target] = jnp.concatenate(
            [
                along[group * rows : (group + 1) * rows, :, target * slab : (target + 1) * slab]
                for group in range(groups)
            ],
            axis=-1,
        )
    pl.semaphore_wait(barrier, count_x + count_y - 2)

    def to_x(kind, source, target):
        copies = []
        for offset in range(1, count_x):
            to = lax.rem(me_x + offset, count_x)
            copies.append(
                pltpu.make_async_remote_copy(
                    src_ref=source.at[to] if source is not total_ref else source,
                    dst_ref=target.at[me_x],
                    send_sem=sems_x.at[kind, 0, offset],
                    recv_sem=sems_x.at[kind, 1, offset],
                    device_id={"gx": to},
                    device_id_type=pl.DeviceIdType.MESH,
                )
            )
        for copy in copies:
            copy.start()
        return copies

    copies_a = to_x(0, send_a, recv_a)
    copies_t = to_x(1, total_ref, totals)
    recv_a[me_x] = send_a[me_x]

    lane = lax.broadcasted_iota(jnp.int32, (full_x, lanes), 1)
    group_of = lane // slab
    decay = decay_ref[...]
    gain = gain_ref[...]
    zero = gain == 0.0

    def power(base, count):
        result = None
        while count:
            if count & 1:
                result = base if result is None else result * base
            count >>= 1
            if count:
                base = base * base
        return result

    def up(value):
        return pltpu.roll(value, slab, 1)

    def down(value):
        return pltpu.roll(value, lanes - slab, 1)

    decay_rows = power(decay, rows)
    decay_block = power(decay_rows, groups)
    decay_full = power(decay_block, count_y)

    for copy in copies_a:
        copy.wait()
    gathered = jnp.concatenate(
        [
            jnp.concatenate([recv_a[place, row] for place in range(count_x)], axis=0)
            for row in range(rows)
        ],
        axis=1,
    )
    modes = dot_split(tx_ref[...], gathered)
    for row in range(rows):
        hat[row] = modes[:, row * lanes : (row + 1) * lanes]

    forward = hat[0]
    for row in range(1, rows):
        forward = decay * forward + hat[row]
    backward = hat[rows - 1]
    for row in range(rows - 2, -1, -1):
        backward = decay * backward + hat[row]
    forward_block = forward
    for group in range(1, groups):
        forward_block = jnp.where(
            group_of == group, forward + decay_rows * up(forward_block), forward_block
        )
    backward_block = backward
    for group in range(groups - 2, -1, -1):
        backward_block = jnp.where(
            group_of == group, backward + decay_rows * down(backward_block), backward_block
        )
    sums[me_y] = jnp.where(group_of == 0, backward_block, forward_block)
    copies_s = []
    for offset in range(1, count_y):
        copies_s.append(
            pltpu.make_async_remote_copy(
                src_ref=sums.at[me_y],
                dst_ref=sums.at[me_y],
                send_sem=sems_y.at[0, offset],
                recv_sem=sems_y.at[1, offset],
                device_id={"gy": lax.rem(me_y + offset, count_y)},
                device_id_type=pl.DeviceIdType.MESH,
            )
        )
    for copy in copies_s:
        copy.start()
    for copy in copies_s:
        copy.wait()

    from_low = jnp.zeros_like(decay)
    all_low = jnp.zeros_like(decay)
    power_low = jnp.ones_like(decay)
    from_high = jnp.zeros_like(decay)
    all_high = jnp.zeros_like(decay)
    power_high = jnp.ones_like(decay)
    for place in range(count_y):
        part = sums[place]
        all_low = all_low * decay_block + part
        from_low = jnp.where(place < me_y, from_low * decay_block + part, from_low)
        power_low = jnp.where(place < me_y, power_low * decay_block, power_low)
        other = count_y - 1 - place
        part = sums[other]
        all_high = all_high * decay_block + part
        from_high = jnp.where(other > me_y, from_high * decay_block + part, from_high)
        power_high = jnp.where(other > me_y, power_high * decay_block, power_high)
    first = group_of == 0

    def swap(value):
        return up(value) if groups == 2 else jnp.where(first, up(value), down(value))

    whole = jnp.where(first, all_high, all_low)
    image = jnp.where(
        zero,
        0.0,
        (whole + decay_full * swap(whole)) / jnp.where(zero, 1.0, 1.0 - decay_full * decay_full),
    )
    entering = jnp.where(first, from_high, from_low) + jnp.where(
        first, power_high, power_low
    ) * swap(image)
    carry_up = up(entering)
    for group in range(1, groups):
        carry_up = jnp.where(group_of == group, up(forward + decay_rows * carry_up), carry_up)
    carry_down = down(entering)
    for group in range(groups - 2, -1, -1):
        carry_down = jnp.where(
            group_of == group, down(backward + decay_rows * carry_down), carry_down
        )

    top = slice(0, 8)
    mean = jnp.where(first, whole, up(whole))
    for group in range(2, groups):
        mean = jnp.where(group_of == group, up(mean), mean)
    mean = mean[top] * (1.0 / (block_y * count_y))
    flat = jnp.zeros_like(mean)
    flats = [flat]
    position = (me_y * block_y + group_of[top] * rows).astype(jnp.float32)
    ahead = carry_up
    left = [ahead]
    for row in range(rows):
        ahead = decay * ahead + hat[row]
        left.append(ahead)
        flat = flat + (ahead[top] - (position + (row + 1.0)) * mean)
        flats.append(flat)
    offset_flat = jnp.zeros_like(mean)
    for group in range(1, groups):
        offset_flat = jnp.where(
            group_of[top] == group, up(offset_flat + flats[rows]), offset_flat
        )
    behind = carry_down
    pressures = [None] * (rows + 1)
    for row in range(rows, -1, -1):
        if row < rows:
            behind = decay * behind + hat[row]
        pressure = gain * (decay * left[row] + behind)
        special = jnp.where(zero[top], flats[row] + offset_flat, pressure[top])
        pressures[row] = jnp.concatenate([special, pressure[8:]], axis=0)
    back = dot_split(txt_ref[...], jnp.concatenate(pressures, axis=1))
    for target in range(count_x):
        for row in range(rows + 1):
            columns = slice(row * lanes, (row + 1) * lanes)
            send_b[target, row] = back[target * block_x : (target + 1) * block_x, columns]
            if target < count_x - 1:
                after = (target + 1) * block_x
                send_e[target, row : row + 1, :] = back[after : after + 1, columns]
        if target == count_x - 1:
            send_e[target] = jnp.zeros(send_e.shape[1:], jnp.float32)
    copies_b = to_x(2, send_b, recv_b)
    copies_e = to_x(3, send_e, recv_e)
    recv_b[me_x] = send_b[me_x]
    recv_e[me_x] = send_e[me_x]
    for copy in copies_t:
        copy.wait()
    before = jnp.zeros_like(before_ref)
    for place in range(count_x - 1):
        before = jnp.where(place < me_x, before + totals[place], before)
    before_ref[...] = before
    for copy in copies_b + copies_e:
        copy.wait()

    def spread(ref):
        parts = []
        for group in range(groups):
            size = rows + (group == groups - 1)
            parts.append(
                jnp.concatenate(
                    [
                        ref[place][:size, ..., group * slab : (group + 1) * slab]
                        for place in range(count_x)
                    ],
                    axis=-1,
                )
            )
        return parts

    table = tz_ref[...]
    field = jnp.concatenate(spread(recv_b), axis=0)
    field = dot_split(field.reshape((block_y + 1) * block_x, length_z), table)
    field = field.reshape(block_y + 1, block_x, length_z)
    for group, part in enumerate(spread(recv_e)):
        edge[group * rows : group * rows + part.shape[0], :] = part
    following = dot_split(edge[...], table)[:block_y]
    middle = field[:block_y]
    last_x = lax.broadcasted_iota(jnp.int32, middle.shape, 1) == block_x - 1
    ahead_x = jnp.where(last_x, following[:, None, :], jnp.roll(middle, -1, axis=1))
    ahead_z = pltpu.roll(middle, length_z - 1, 2)
    gradients = (ahead_x - middle, field[1:] - middle, ahead_z - middle)
    place_x = lax.broadcasted_iota(jnp.int32, div_ref.shape, 0) + me_x * block_x
    place_y = lax.broadcasted_iota(jnp.int32, div_ref.shape, 1) + me_y * block_y
    place_z = lax.broadcasted_iota(jnp.int32, div_ref.shape, 2)
    opened = (
        place_x < full_x - 1,
        place_y < block_y * count_y - 1,
        place_z < length_z - 1,
    )
    for axis_id in range(3):
        value = lifted_ref[axis_id] - jnp.swapaxes(gradients[axis_id], 0, 1)
        out_ref[axis_id] = jnp.where(opened[axis_id], value, 0.0)


def pressure_solve(divergence, lifted, total):
    block_x, block_y, length_z = divergence.shape
    count_x = lax.axis_size("gx")
    count_y = lax.axis_size("gy")
    full_x = block_x * count_x
    slab = length_z // count_x
    lanes = 128
    groups = lanes // slab
    rows = block_y // groups
    padded = -(-(rows + 1) // 8) * 8
    table_z = cosine_table(length_z)
    table_x = cosine_table(full_x)
    decay, gain = mode_tables(full_x, length_z, slab, groups, lax.axis_index("gx") * slab)
    vmem = pl.BlockSpec(memory_space=pltpu.VMEM)

    def buffer(*shape):
        return pltpu.VMEM(shape, jnp.float32)

    return pl.pallas_call(
        functools.partial(solve_kernel, count_x, count_y),
        out_shape=(
            jax.ShapeDtypeStruct(lifted.shape, jnp.float32),
            jax.ShapeDtypeStruct(total.shape, jnp.float32),
        ),
        in_specs=[vmem] * 9,
        out_specs=(vmem, vmem),
        scratch_shapes=[
            buffer(count_x, rows, block_x, lanes),
            buffer(count_x, rows, block_x, lanes),
            buffer(count_x, rows + 1, block_x, lanes),
            buffer(count_x, rows + 1, block_x, lanes),
            buffer(count_x, padded, lanes),
            buffer(count_x, padded, lanes),
            buffer(block_y + 8, length_z),
            buffer(count_x, *total.shape),
            buffer(count_y, full_x, lanes),
            buffer(rows, full_x, lanes),
            pltpu.SemaphoreType.DMA((4, 2, count_x)),
            pltpu.SemaphoreType.DMA((2, count_y)),
        ],
        compiler_params=pltpu.CompilerParams(
            collective_id=0, has_side_effects=True, vmem_limit_bytes=48 * 1024 * 1024
        ),
    )(
        divergence,
        lifted,
        total,
        jnp.asarray(table_z),
        jnp.asarray(table_z.T.copy()),
        jnp.asarray(table_x),
        jnp.asarray(table_x.T.copy()),
        decay,
        gain,
    )


def per_device(velocity, density):
    block_x, block_y, length_z = density.shape
    count_x = lax.axis_size("gx")
    count_y = lax.axis_size("gy")
    full_x = block_x * count_x
    full_y = block_y * count_y
    anchor_x = lax.axis_index("gx") * block_x
    anchor_y = lax.axis_index("gy") * block_y

    def confine(fields, rim_width):
        along_x = anchor_x - rim_width + jnp.arange(block_x + 2 * rim_width)
        along_y = anchor_y - rim_width + jnp.arange(block_y + 2 * rim_width)
        along_z = jnp.arange(length_z)
        inside = ((along_x >= 0) & (along_x < full_x))[:, None, None] & (
            (along_y >= 0) & (along_y < full_y)
        )[None, :, None]
        open_x = inside & (along_x < full_x - 1)[:, None, None]
        open_y = inside & (along_y < full_y - 1)[None, :, None]
        open_z = inside & (along_z < length_z - 1)[None, None, :]
        return jnp.stack(
            [fields[0] * open_x, fields[1] * open_y, fields[2] * open_z, fields[3] * inside]
        )

    fields = jnp.concatenate(
        [velocity.astype(jnp.float32), density.astype(jnp.float32)[None]], axis=0
    )
    widened = advect_halo(fields, 2)
    section_one = confine(fields + time_step * tendency_rim(widened), 0)
    section_one = advect_halo(section_one, 3)
    earlier = cropped(widened, 2, 1)
    section_two = confine(
        0.5 * earlier + 0.5 * (cropped(section_one, 3, 1) + time_step * tendency_rim(section_one)),
        1,
    )
    smoke_now = section_two[3]
    smoke_above = jnp.concatenate(
        [smoke_now[:, :, 1:], jnp.zeros_like(smoke_now[:, :, :1])], axis=2
    )
    lifted = confine(
        jnp.stack(
            [
                section_two[0],
                section_two[1],
                section_two[2] + time_step * buoyancy * 0.5 * (smoke_now + smoke_above),
                smoke_now,
            ]
        ),
        1,
    )
    interior = lifted[:, 1:-1, 1:-1, :]
    below_z = jnp.concatenate(
        [jnp.zeros_like(interior[2][:, :, :1]), interior[2][:, :, :-1]], axis=2
    )
    divergence = (
        interior[0]
        - lifted[0, :-2, 1:-1, :]
        + (interior[1] - lifted[1, 1:-1, :-2, :])
        + (interior[2] - below_z)
    )
    column = interior[3]
    attenuation = extinction / full_x
    running = jnp.cumsum(column, axis=0)
    projected, before = pressure_solve(divergence, interior[:3], running[-1])
    optical = attenuation * (before[None] + running - column)
    emission = jnp.exp(-optical) * -jnp.expm1(-attenuation * column) / attenuation
    return (projected, emission)


def solution(mesh):
    in_specs = (P(None, "gx", "gy", None), P("gx", "gy", None))
    out_specs = (P(None, "gx", "gy", None), P("gx", "gy", None))
    return jax.shard_map(
        per_device, mesh=mesh, in_specs=in_specs, out_specs=out_specs, check_vma=False
    )
```

```python
import functools

import jax
import jax.numpy as jnp
from jax import lax
from jax.experimental import pallas as pl
from jax.experimental.pallas import tpu as pltpu
from jax.sharding import PartitionSpec as P
import numpy as np

time_step = 0.4
buoyancy = 2.0
extinction = 3.0
highest = lax.Precision.HIGHEST


def cosine_table(length):
    modes = np.arange(length)[:, None]
    centres = np.arange(length)[None, :] + 0.5
    factor = np.where(modes == 0, np.sqrt(1.0 / length), np.sqrt(2.0 / length))
    return (factor * np.cos(np.pi * modes * centres / length)).astype(np.float32)


def advect_kernel(
    count_x,
    count_y,
    velocity_ref,
    density_ref,
    lifted_ref,
    smoke_ref,
    div_ref,
    wide,
    middle,
    face_x,
    face_y,
    sent,
    received,
):
    block_x, block_y, length_z = density_ref.shape
    me_x = lax.axis_index("gx")
    me_y = lax.axis_index("gy")
    last_x = block_x * count_x - 1
    last_y = block_y * count_y - 1
    low_y, high_y, rim = 16, 16 + block_y, 8
    moves = (
        (1, 0, (0, 4), (block_x + 1, 1, 4), (low_y, low_y, block_y)),
        (1, 0, (0, 1), (block_x, 0, 1), (low_y, low_y, block_y)),
        (-1, 0, (0, 4), (5, block_x + 5, 4), (low_y, low_y, block_y)),
        (1, 1, (0, 4), (block_x + 1, 1, 4), (high_y - rim, low_y - rim, rim)),
        (1, -1, (0, 4), (block_x + 1, 1, 4), (low_y, high_y, rim)),
        (-1, 1, (0, 4), (5, block_x + 5, 4), (high_y - rim, low_y - rim, rim)),
        (-1, -1, (0, 4), (5, block_x + 5, 4), (low_y, high_y, rim)),
        (0, 1, (0, 4), (5, 5, block_x), (high_y - rim, low_y - rim, rim)),
        (0, -1, (0, 4), (5, 5, block_x), (low_y, high_y, rim)),
    )

    def exists(offset_x, offset_y):
        to_x = me_x + offset_x
        to_y = me_y + offset_y
        return (to_x >= 0) & (to_x < count_x) & (to_y >= 0) & (to_y < count_y)

    def copy_of(index):
        offset_x, offset_y, fields, along_x, along_y = moves[index]
        return pltpu.make_async_remote_copy(
            src_ref=wide.at[
                pl.ds(*fields), pl.ds(along_x[0], along_x[2]), pl.ds(along_y[0], along_y[2])
            ],
            dst_ref=wide.at[
                pl.ds(*fields), pl.ds(along_x[1], along_x[2]), pl.ds(along_y[1], along_y[2])
            ],
            send_sem=sent.at[index],
            recv_sem=received.at[index],
            device_id={"gx": me_x + offset_x, "gy": me_y + offset_y},
            device_id_type=pl.DeviceIdType.MESH,
        )

    around = [(i, j) for i in (-1, 0, 1) for j in (-1, 0, 1) if (i, j) != (0, 0)]
    barrier = pltpu.get_barrier_semaphore()
    for offset_x, offset_y in around:

        @pl.when(exists(offset_x, offset_y))
        def _():
            pl.semaphore_signal(
                barrier,
                inc=1,
                device_id={"gx": me_x + offset_x, "gy": me_y + offset_y},
                device_id_type=pl.DeviceIdType.MESH,
            )

    for field in range(3):
        wide[field, 5 : 5 + block_x, low_y:high_y, :] = velocity_ref[field].astype(jnp.float32)
    wide[3, 5 : 5 + block_x, low_y:high_y, :] = density_ref[...].astype(jnp.float32)
    span_x = 3 - (me_x == 0).astype(jnp.int32) - (me_x == count_x - 1).astype(jnp.int32)
    span_y = 3 - (me_y == 0).astype(jnp.int32) - (me_y == count_y - 1).astype(jnp.int32)
    pl.semaphore_wait(barrier, span_x * span_y - 1)

    for index, move in enumerate(moves):

        @pl.when(exists(move[0], move[1]))
        def _():
            copy_of(index).start()

    for index, move in enumerate(moves):
        fields, along_x, along_y = move[2:]

        @pl.when(jnp.logical_not(exists(-move[0], -move[1])))
        def _():
            shape = (fields[1], along_x[2], along_y[2], length_z)
            wide[
                0 : fields[1],
                along_x[1] : along_x[1] + along_x[2],
                along_y[1] : along_y[1] + along_y[2],
                :,
            ] = jnp.zeros(shape, jnp.float32)

    def arrive(indices):
        for index in indices:

            @pl.when(exists(-moves[index][0], -moves[index][1]))
            def _():
                copy_of(index).wait_recv()

    lane = lax.broadcasted_iota(jnp.int32, (8, length_z), 1)
    line = lax.broadcasted_iota(jnp.int32, (8, length_z), 0)
    scale = -time_step / 12.0

    def advance(source, at_x, at_y, fields):
        centres = [source[field, at_x, at_y : at_y + 8, :] for field in range(4)]
        weights = []
        base = None
        for axis_id in range(3):
            speed = scale * centres[axis_id]
            size = jnp.abs(speed)
            eight = 8.0 * speed
            four = 4.0 * size
            parts = {1: four + eight, -1: four - eight, 2: -speed - size, -2: speed - size}
            if axis_id == 2:
                parts[1] = jnp.where(lane < length_z - 1, parts[1], 0.0)
                parts[2] = jnp.where(lane < length_z - 2, parts[2], 0.0)
                parts[-1] = jnp.where(lane > 0, parts[-1], 0.0)
                parts[-2] = jnp.where(lane > 1, parts[-2], 0.0)
            weights.append(parts)
            base = size if base is None else base + size
        base = 1.0 - 6.0 * base
        results = []
        for field in fields:
            total = centres[field] * base
            for offset in (-2, -1, 1, 2):
                total = total + weights[0][offset] * source[
                    field, at_x + offset, at_y : at_y + 8, :
                ]
                total = total + weights[1][offset] * source[
                    field, at_x, at_y + offset : at_y + offset + 8, :
                ]
                total = total + weights[2][offset] * pltpu.roll(
                    centres[field], (-offset) % length_z, 1
                )
            results.append(total)
        return results

    def walled(field, value, at_x, at_y):
        if field == 0:
            return value * jnp.where(me_x * block_x + at_x == last_x, 0.0, 1.0)
        if field == 1:
            return jnp.where(me_y * block_y + at_y + line == last_y, 0.0, value)
        if field == 2:
            return jnp.where(lane == length_z - 1, 0.0, value)
        return value

    def first_rows(start, stop, fields=(0, 1, 2, 3), tiles=None):
        tiles = range(low_y - rim, high_y + rim, 8) if tiles is None else tiles

        def row(at, carry):
            for at_y in tiles:
                values = advance(wide, at + 2, at_y, fields)
                for field, value in zip(fields, values):
                    middle[field, at, at_y : at_y + 8, :] = walled(
                        field, value, at - 3, at_y - low_y
                    )
            return carry

        lax.fori_loop(start + 3, stop + 3, row, 0)

    def second(at_x, at_y, fields):
        values = advance(middle, at_x + 3, at_y, fields)
        return [
            0.5 * wide[field, at_x + 5, at_y : at_y + 8, :] + 0.5 * value
            for field, value in zip(fields, values)
        ]

    inside = range(low_y, high_y, 8)

    def second_rows(start, stop):
        def row(at_x, carry):
            (value,) = second(at_x, low_y - 8, (1,))
            face_y[at_x, 0:8, :] = walled(1, value, at_x, -8)
            for at_y in inside:
                near = at_y - low_y
                part_x, part_y, part_z, smoke = second(at_x, at_y, (0, 1, 2, 3))
                above = pltpu.roll(smoke, length_z - 1, 1)
                part_z = part_z + (time_step * buoyancy * 0.5) * (smoke + above)
                face_x[at_x + 1, near : near + 8, :] = walled(0, part_x, at_x, near)
                face_y[at_x, near + 8 : near + 16, :] = walled(1, part_y, at_x, near)
                lifted_ref[2, at_x, near : near + 8, :] = walled(2, part_z, at_x, near)
                smoke_ref[at_x, near : near + 8, :] = smoke
            return carry

        lax.fori_loop(start, stop, row, 0)

    arrive((7, 8))
    first_rows(2, block_x - 2)
    second_rows(4, block_x - 4)
    arrive(range(7))
    first_rows(-3, -2, (0,), inside)
    first_rows(-2, 2)
    first_rows(block_x - 2, block_x + 2)
    for at_y in inside:
        (value,) = second(-1, at_y, (0,))
        face_x[0, at_y - low_y : at_y - low_y + 8, :] = walled(0, value, -1, 0)
    second_rows(0, 4)
    second_rows(block_x - 4, block_x)

    def differ(at_x, carry):
        part_x = face_x[at_x + 1]
        part_y = face_y[at_x, 8 : 8 + block_y, :]
        part_z = lifted_ref[2, at_x]
        below = jnp.where(
            lax.broadcasted_iota(jnp.int32, part_z.shape, 1) > 0, pltpu.roll(part_z, 1, 1), 0.0
        )
        lifted_ref[0, at_x] = part_x
        lifted_ref[1, at_x] = part_y
        div_ref[at_x] = (
            part_x
            - face_x[at_x]
            + (part_y - face_y[at_x, 7 : 7 + block_y, :])
            + (part_z - below)
        )
        return carry

    lax.fori_loop(0, block_x, differ, 0)
    for index, move in enumerate(moves):

        @pl.when(exists(move[0], move[1]))
        def _():
            copy_of(index).wait_send()


def advect(velocity, density):
    block_x, block_y, length_z = density.shape
    count_x = lax.axis_size("gx")
    count_y = lax.axis_size("gy")
    vmem = pl.BlockSpec(memory_space=pltpu.VMEM)

    def buffer(*shape):
        return pltpu.VMEM(shape, jnp.float32)

    def result(*shape):
        return jax.ShapeDtypeStruct(shape, jnp.float32)

    return pl.pallas_call(
        functools.partial(advect_kernel, count_x, count_y),
        out_shape=(
            result(3, *density.shape),
            result(*density.shape),
            result(*density.shape),
        ),
        in_specs=[vmem] * 2,
        out_specs=(vmem,) * 3,
        scratch_shapes=[
            buffer(4, block_x + 9, block_y + 32, length_z),
            buffer(4, block_x + 5, block_y + 32, length_z),
            buffer(block_x + 1, block_y, length_z),
            buffer(block_x, block_y + 8, length_z),
            pltpu.SemaphoreType.DMA((9,)),
            pltpu.SemaphoreType.DMA((9,)),
        ],
        compiler_params=pltpu.CompilerParams(
            collective_id=1, has_side_effects=True, vmem_limit_bytes=48 * 1024 * 1024
        ),
    )(velocity, density)


def halves(value):
    big = value.astype(jnp.bfloat16)
    return big, (value - big.astype(jnp.float32)).astype(jnp.bfloat16)


def dot_split(left, right):
    left_big, left_rest = halves(left)
    right_big, right_rest = halves(right)

    def dot(one, two):
        return jnp.dot(one, two, preferred_element_type=jnp.float32)

    return dot(left_big, right_big) + (dot(left_big, right_rest) + dot(left_rest, right_big))


def dot_full(left, right):
    return jnp.dot(left, right, precision=highest, preferred_element_type=jnp.float32)


def mode_tables(full_x, length_z, slab, groups, anchor_kz):
    modes_x = jnp.arange(full_x, dtype=jnp.float32)[:, None]
    modes_z = (anchor_kz + jnp.arange(slab * groups) % slab).astype(jnp.float32)[None, :]
    shift = 4.0 * (
        jnp.sin(modes_x * (np.pi / (2 * full_x))) ** 2
        + jnp.sin(modes_z * (np.pi / (2 * length_z))) ** 2
    )
    root = jnp.sqrt(shift + 0.25 * shift * shift)
    decay = 1.0 / (1.0 + 0.5 * shift + root)
    zero = (modes_x == 0) & (modes_z == 0)
    gain = jnp.where(zero, 0.0, -0.5 / jnp.where(zero, 1.0, root))
    return decay, gain


def solve_kernel(
    count_x,
    count_y,
    div_ref,
    lifted_ref,
    total_ref,
    tz_ref,
    tzt_ref,
    tx_ref,
    txt_ref,
    decay_ref,
    gain_ref,
    out_ref,
    before_ref,
    send_a,
    recv_a,
    send_b,
    recv_b,
    send_e,
    recv_e,
    edge,
    totals,
    sums,
    hat,
    sems_x,
    sems_y,
):
    block_x, block_y, length_z = div_ref.shape
    full_x = block_x * count_x
    me_x = lax.axis_index("gx")
    me_y = lax.axis_index("gy")
    slab = length_z // count_x
    lanes = recv_a.shape[-1]
    groups = lanes // slab
    rows = block_y // groups

    barrier = pltpu.get_barrier_semaphore()
    for offset in range(1, count_x):
        pl.semaphore_signal(
            barrier,
            inc=1,
            device_id={"gx": lax.rem(me_x + offset, count_x)},
            device_id_type=pl.DeviceIdType.MESH,
        )
    for offset in range(1, count_y):
        pl.semaphore_signal(
            barrier,
            inc=1,
            device_id={"gy": lax.rem(me_y + offset, count_y)},
            device_id_type=pl.DeviceIdType.MESH,
        )
    div = jnp.swapaxes(div_ref[...], 0, 1).reshape(block_y * block_x, length_z)
    along = dot_split(div, tzt_ref[...]).reshape(block_y, block_x, length_z)
    for target in range(count_x):
        send_a[target] = jnp.concatenate(
            [
                along[group * rows : (group + 1) * rows, :, target * slab : (target + 1) * slab]
                for group in range(groups)
            ],
            axis=-1,
        )
    pl.semaphore_wait(barrier, count_x + count_y - 2)

    def to_x(kind, source, target):
        copies = []
        for offset in range(1, count_x):
            to = lax.rem(me_x + offset, count_x)
            copies.append(
                pltpu.make_async_remote_copy(
                    src_ref=source.at[to] if source is not total_ref else source,
                    dst_ref=target.at[me_x],
                    send_sem=sems_x.at[kind, 0, offset],
                    recv_sem=sems_x.at[kind, 1, offset],
                    device_id={"gx": to},
                    device_id_type=pl.DeviceIdType.MESH,
                )
            )
        for copy in copies:
            copy.start()
        return copies

    copies_a = to_x(0, send_a, recv_a)
    copies_t = to_x(1, total_ref, totals)
    recv_a[me_x] = send_a[me_x]

    lane = lax.broadcasted_iota(jnp.int32, (full_x, lanes), 1)
    group_of = lane // slab
    decay = decay_ref[...]
    gain = gain_ref[...]
    zero = gain == 0.0

    def power(base, count):
        result = None
        while count:
            if count & 1:
                result = base if result is None else result * base
            count >>= 1
            if count:
                base = base * base
        return result

    def up(value):
        return pltpu.roll(value, slab, 1)

    def down(value):
        return pltpu.roll(value, lanes - slab, 1)

    decay_rows = power(decay, rows)
    decay_block = power(decay_rows, groups)
    decay_full = power(decay_block, count_y)

    for copy in copies_a:
        copy.wait()
    gathered = jnp.concatenate(
        [
            jnp.concatenate([recv_a[place, row] for place in range(count_x)], axis=0)
            for row in range(rows)
        ],
        axis=1,
    )
    modes = dot_split(tx_ref[...], gathered)
    for row in range(rows):
        hat[row] = modes[:, row * lanes : (row + 1) * lanes]

    forward = hat[0]
    for row in range(1, rows):
        forward = decay * forward + hat[row]
    backward = hat[rows - 1]
    for row in range(rows - 2, -1, -1):
        backward = decay * backward + hat[row]
    forward_block = forward
    for group in range(1, groups):
        forward_block = jnp.where(
            group_of == group, forward + decay_rows * up(forward_block), forward_block
        )
    backward_block = backward
    for group in range(groups - 2, -1, -1):
        backward_block = jnp.where(
            group_of == group, backward + decay_rows * down(backward_block), backward_block
        )
    sums[me_y] = jnp.where(group_of == 0, backward_block, forward_block)
    copies_s = []
    for offset in range(1, count_y):
        copies_s.append(
            pltpu.make_async_remote_copy(
                src_ref=sums.at[me_y],
                dst_ref=sums.at[me_y],
                send_sem=sems_y.at[0, offset],
                recv_sem=sems_y.at[1, offset],
                device_id={"gy": lax.rem(me_y + offset, count_y)},
                device_id_type=pl.DeviceIdType.MESH,
            )
        )
    for copy in copies_s:
        copy.start()
    for copy in copies_s:
        copy.wait()

    from_low = jnp.zeros_like(decay)
    all_low = jnp.zeros_like(decay)
    power_low = jnp.ones_like(decay)
    from_high = jnp.zeros_like(decay)
    all_high = jnp.zeros_like(decay)
    power_high = jnp.ones_like(decay)
    for place in range(count_y):
        part = sums[place]
        all_low = all_low * decay_block + part
        from_low = jnp.where(place < me_y, from_low * decay_block + part, from_low)
        power_low = jnp.where(place < me_y, power_low * decay_block, power_low)
        other = count_y - 1 - place
        part = sums[other]
        all_high = all_high * decay_block + part
        from_high = jnp.where(other > me_y, from_high * decay_block + part, from_high)
        power_high = jnp.where(other > me_y, power_high * decay_block, power_high)
    first = group_of == 0

    def swap(value):
        return up(value) if groups == 2 else jnp.where(first, up(value), down(value))

    whole = jnp.where(first, all_high, all_low)
    image = jnp.where(
        zero,
        0.0,
        (whole + decay_full * swap(whole)) / jnp.where(zero, 1.0, 1.0 - decay_full * decay_full),
    )
    entering = jnp.where(first, from_high, from_low) + jnp.where(
        first, power_high, power_low
    ) * swap(image)
    carry_up = up(entering)
    for group in range(1, groups):
        carry_up = jnp.where(group_of == group, up(forward + decay_rows * carry_up), carry_up)
    carry_down = down(entering)
    for group in range(groups - 2, -1, -1):
        carry_down = jnp.where(
            group_of == group, down(backward + decay_rows * carry_down), carry_down
        )

    top = slice(0, 8)
    mean = jnp.where(first, whole, up(whole))
    for group in range(2, groups):
        mean = jnp.where(group_of == group, up(mean), mean)
    mean = mean[top] * (1.0 / (block_y * count_y))
    flat = jnp.zeros_like(mean)
    flats = [flat]
    position = (me_y * block_y + group_of[top] * rows).astype(jnp.float32)
    ahead = carry_up
    left = [ahead]
    for row in range(rows):
        ahead = decay * ahead + hat[row]
        left.append(ahead)
        flat = flat + (ahead[top] - (position + (row + 1.0)) * mean)
        flats.append(flat)
    offset_flat = jnp.zeros_like(mean)
    for group in range(1, groups):
        offset_flat = jnp.where(
            group_of[top] == group, up(offset_flat + flats[rows]), offset_flat
        )
    behind = carry_down
    pressures = [None] * (rows + 1)
    for row in range(rows, -1, -1):
        if row < rows:
            behind = decay * behind + hat[row]
        pressure = gain * (decay * left[row] + behind)
        special = jnp.where(zero[top], flats[row] + offset_flat, pressure[top])
        pressures[row] = jnp.concatenate([special, pressure[8:]], axis=0)
    back = dot_full(txt_ref[...], jnp.concatenate(pressures, axis=1))
    for target in range(count_x):
        for row in range(rows + 1):
            columns = slice(row * lanes, (row + 1) * lanes)
            send_b[target, row] = back[target * block_x : (target + 1) * block_x, columns]
            if target < count_x - 1:
                after = (target + 1) * block_x
                send_e[target, row : row + 1, :] = back[after : after + 1, columns]
        if target == count_x - 1:
            send_e[target] = jnp.zeros(send_e.shape[1:], jnp.float32)
    copies_b = to_x(2, send_b, recv_b)
    copies_e = to_x(3, send_e, recv_e)
    recv_b[me_x] = send_b[me_x]
    recv_e[me_x] = send_e[me_x]
    for copy in copies_t:
        copy.wait()
    before = jnp.zeros_like(before_ref)
    for place in range(count_x - 1):
        before = jnp.where(place < me_x, before + totals[place], before)
    before_ref[...] = before
    for copy in copies_b + copies_e:
        copy.wait()

    def spread(ref):
        parts = []
        for group in range(groups):
            size = rows + (group == groups - 1)
            parts.append(
                jnp.concatenate(
                    [
                        ref[place][:size, ..., group * slab : (group + 1) * slab]
                        for place in range(count_x)
                    ],
                    axis=-1,
                )
            )
        return parts

    table = tz_ref[...]
    field = jnp.concatenate(spread(recv_b), axis=0)
    field = dot_full(field.reshape((block_y + 1) * block_x, length_z), table)
    field = field.reshape(block_y + 1, block_x, length_z)
    for group, part in enumerate(spread(recv_e)):
        edge[group * rows : group * rows + part.shape[0], :] = part
    following = dot_full(edge[...], table)[:block_y]
    middle = field[:block_y]
    last_x = lax.broadcasted_iota(jnp.int32, middle.shape, 1) == block_x - 1
    ahead_x = jnp.where(last_x, following[:, None, :], jnp.roll(middle, -1, axis=1))
    ahead_z = pltpu.roll(middle, length_z - 1, 2)
    gradients = (ahead_x - middle, field[1:] - middle, ahead_z - middle)
    place_x = lax.broadcasted_iota(jnp.int32, div_ref.shape, 0) + me_x * block_x
    place_y = lax.broadcasted_iota(jnp.int32, div_ref.shape, 1) + me_y * block_y
    place_z = lax.broadcasted_iota(jnp.int32, div_ref.shape, 2)
    opened = (
        place_x < full_x - 1,
        place_y < block_y * count_y - 1,
        place_z < length_z - 1,
    )
    for axis_id in range(3):
        value = lifted_ref[axis_id] - jnp.swapaxes(gradients[axis_id], 0, 1)
        out_ref[axis_id] = jnp.where(opened[axis_id], value, 0.0)


def pressure_solve(divergence, lifted, total):
    block_x, block_y, length_z = divergence.shape
    count_x = lax.axis_size("gx")
    count_y = lax.axis_size("gy")
    full_x = block_x * count_x
    slab = length_z // count_x
    lanes = 128
    groups = lanes // slab
    rows = block_y // groups
    padded = -(-(rows + 1) // 8) * 8
    table_z = cosine_table(length_z)
    table_x = cosine_table(full_x)
    decay, gain = mode_tables(full_x, length_z, slab, groups, lax.axis_index("gx") * slab)
    vmem = pl.BlockSpec(memory_space=pltpu.VMEM)

    def buffer(*shape):
        return pltpu.VMEM(shape, jnp.float32)

    return pl.pallas_call(
        functools.partial(solve_kernel, count_x, count_y),
        out_shape=(
            jax.ShapeDtypeStruct(lifted.shape, jnp.float32),
            jax.ShapeDtypeStruct(total.shape, jnp.float32),
        ),
        in_specs=[vmem] * 9,
        out_specs=(vmem, vmem),
        scratch_shapes=[
            buffer(count_x, rows, block_x, lanes),
            buffer(count_x, rows, block_x, lanes),
            buffer(count_x, rows + 1, block_x, lanes),
            buffer(count_x, rows + 1, block_x, lanes),
            buffer(count_x, padded, lanes),
            buffer(count_x, padded, lanes),
            buffer(block_y + 8, length_z),
            buffer(count_x, *total.shape),
            buffer(count_y, full_x, lanes),
            buffer(rows, full_x, lanes),
            pltpu.SemaphoreType.DMA((4, 2, count_x)),
            pltpu.SemaphoreType.DMA((2, count_y)),
        ],
        compiler_params=pltpu.CompilerParams(
            collective_id=0, has_side_effects=True, vmem_limit_bytes=48 * 1024 * 1024
        ),
    )(
        divergence,
        lifted,
        total,
        jnp.asarray(table_z),
        jnp.asarray(table_z.T.copy()),
        jnp.asarray(table_x),
        jnp.asarray(table_x.T.copy()),
        decay,
        gain,
    )


def per_device(velocity, density):
    lifted, column, divergence = advect(velocity, density)
    attenuation = extinction / (density.shape[0] * lax.axis_size("gx"))
    running = jnp.cumsum(column, axis=0)
    projected, before = pressure_solve(divergence, lifted, running[-1])
    optical = attenuation * (before[None] + running - column)
    emission = jnp.exp(-optical) * -jnp.expm1(-attenuation * column) / attenuation
    return (projected, emission)


def solution(mesh):
    in_specs = (P(None, "gx", "gy", None), P("gx", "gy", None))
    out_specs = (P(None, "gx", "gy", None), P("gx", "gy", None))
    return jax.shard_map(
        per_device, mesh=mesh, in_specs=in_specs, out_specs=out_specs, check_vma=False
    )
```

```python
import functools

import jax
import jax.numpy as jnp
from jax import lax
from jax.experimental import pallas as pl
from jax.experimental.pallas import tpu as pltpu
from jax.sharding import PartitionSpec as P
import numpy as np

time_step = 0.4
buoyancy = 2.0
extinction = 3.0
highest = lax.Precision.HIGHEST


def cosine_table(length):
    modes = np.arange(length)[:, None]
    centres = np.arange(length)[None, :] + 0.5
    factor = np.where(modes == 0, np.sqrt(1.0 / length), np.sqrt(2.0 / length))
    return (factor * np.cos(np.pi * modes * centres / length)).astype(np.float32)


def advect_part(
    count_x,
    count_y,
    meet,
    velocity_ref,
    density_ref,
    lifted_ref,
    smoke_ref,
    div_ref,
    wide,
    middle,
    face_x,
    face_y,
    sent,
    received,
):
    block_x, block_y, length_z = density_ref.shape
    me_x = lax.axis_index("gx")
    me_y = lax.axis_index("gy")
    last_x = block_x * count_x - 1
    last_y = block_y * count_y - 1
    low_y, high_y, rim = 16, 16 + block_y, 8
    full = (low_y, low_y, block_y)
    upward = (high_y - rim, low_y - rim, rim)
    downward = (low_y, high_y, rim)
    moves = (
        (1, 0, (0, 4), (block_x, 0, 2), full),
        (-1, 0, (0, 4), (2, block_x + 2, 2), full),
        (0, 1, (0, 4), (2, 2, block_x), upward),
        (0, -1, (0, 4), (2, 2, block_x), downward),
        (1, 0, (0, 4), (block_x + 1, 1, 2), full),
        (-1, 0, (0, 4), (3, block_x + 3, 2), full),
        (1, 0, (0, 1), (block_x, 0, 1), full),
        (1, 1, (0, 2), (block_x + 1, 1, 2), upward),
        (1, -1, (0, 1), (block_x + 2, 2, 1), downward),
        (-1, 1, (1, 1), (3, block_x + 3, 2), upward),
        (0, 1, (0, 4), (3, 3, block_x), upward),
        (0, -1, (0, 4), (3, 3, block_x), downward),
    )

    def array_of(index):
        return wide if index < 4 else middle

    def exists(offset_x, offset_y):
        to_x = me_x + offset_x
        to_y = me_y + offset_y
        return (to_x >= 0) & (to_x < count_x) & (to_y >= 0) & (to_y < count_y)

    def copy_of(index):
        offset_x, offset_y, fields, along_x, along_y = moves[index]
        return pltpu.make_async_remote_copy(
            src_ref=array_of(index).at[
                pl.ds(*fields), pl.ds(along_x[0], along_x[2]), pl.ds(along_y[0], along_y[2])
            ],
            dst_ref=array_of(index).at[
                pl.ds(*fields), pl.ds(along_x[1], along_x[2]), pl.ds(along_y[1], along_y[2])
            ],
            send_sem=sent.at[index],
            recv_sem=received.at[index],
            device_id={"gx": me_x + offset_x, "gy": me_y + offset_y},
            device_id_type=pl.DeviceIdType.MESH,
        )

    for field in range(3):
        wide[field, 2 : 2 + block_x, low_y:high_y, :] = velocity_ref[field].astype(jnp.float32)
    wide[3, 2 : 2 + block_x, low_y:high_y, :] = density_ref[...].astype(jnp.float32)
    meet()

    def depart(indices):
        for index in indices:

            @pl.when(exists(moves[index][0], moves[index][1]))
            def _():
                copy_of(index).start()

    depart(range(4))
    for index, move in enumerate(moves):
        fields, along_x, along_y = move[2:]

        @pl.when(jnp.logical_not(exists(-move[0], -move[1])))
        def _():
            shape = (fields[1], along_x[2], along_y[2], length_z)
            array_of(index)[
                fields[0] : fields[0] + fields[1],
                along_x[1] : along_x[1] + along_x[2],
                along_y[1] : along_y[1] + along_y[2],
                :,
            ] = jnp.zeros(shape, jnp.float32)

    def arrive(indices):
        for index in indices:

            @pl.when(exists(-moves[index][0], -moves[index][1]))
            def _():
                copy_of(index).wait_recv()

    lane = lax.broadcasted_iota(jnp.int32, (8, length_z), 1)
    line = lax.broadcasted_iota(jnp.int32, (8, length_z), 0)
    scale = -time_step / 12.0

    def advance(source, at_x, at_y, fields):
        centres = [source[field, at_x, at_y : at_y + 8, :] for field in range(4)]
        weights = []
        base = None
        for axis_id in range(3):
            speed = scale * centres[axis_id]
            size = jnp.abs(speed)
            eight = 8.0 * speed
            four = 4.0 * size
            parts = {1: four + eight, -1: four - eight, 2: -speed - size, -2: speed - size}
            if axis_id == 2:
                parts[1] = jnp.where(lane < length_z - 1, parts[1], 0.0)
                parts[2] = jnp.where(lane < length_z - 2, parts[2], 0.0)
                parts[-1] = jnp.where(lane > 0, parts[-1], 0.0)
                parts[-2] = jnp.where(lane > 1, parts[-2], 0.0)
            weights.append(parts)
            base = size if base is None else base + size
        base = 1.0 - 6.0 * base
        results = []
        for field in fields:
            total = centres[field] * base
            for offset in (-2, -1, 1, 2):
                total = total + weights[0][offset] * source[
                    field, at_x + offset, at_y : at_y + 8, :
                ]
                total = total + weights[1][offset] * source[
                    field, at_x, at_y + offset : at_y + offset + 8, :
                ]
                total = total + weights[2][offset] * pltpu.roll(
                    centres[field], (-offset) % length_z, 1
                )
            results.append(total)
        return results

    def walled(field, value, at_x, at_y):
        if field == 0:
            return value * jnp.where(me_x * block_x + at_x == last_x, 0.0, 1.0)
        if field == 1:
            return jnp.where(me_y * block_y + at_y + line == last_y, 0.0, value)
        if field == 2:
            return jnp.where(lane == length_z - 1, 0.0, value)
        return value

    inside = tuple(range(low_y, high_y, 8))

    def first_rows(start, stop, tiles=inside):
        def row(at_x, carry):
            for at_y in tiles:
                values = advance(wide, at_x + 2, at_y, (0, 1, 2, 3))
                for field, value in enumerate(values):
                    middle[field, at_x + 3, at_y : at_y + 8, :] = walled(
                        field, value, at_x, at_y - low_y
                    )
            return carry

        lax.fori_loop(start, stop, row, 0)

    def second(at_x, at_y, fields):
        values = advance(middle, at_x + 3, at_y, fields)
        return [
            0.5 * wide[field, at_x + 2, at_y : at_y + 8, :] + 0.5 * value
            for field, value in zip(fields, values)
        ]

    def second_rows(start, stop, tiles=inside):
        def row(at_x, carry):
            if inside[0] in tiles:
                (value,) = second(at_x, low_y - 8, (1,))
                face_y[at_x, 0:8, :] = walled(1, value, at_x, -8)
            for at_y in tiles:
                near = at_y - low_y
                part_x, part_y, part_z, smoke = second(at_x, at_y, (0, 1, 2, 3))
                above = pltpu.roll(smoke, length_z - 1, 1)
                part_z = part_z + (time_step * buoyancy * 0.5) * (smoke + above)
                face_x[at_x + 1, near : near + 8, :] = walled(0, part_x, at_x, near)
                face_y[at_x, near + 8 : near + 16, :] = walled(1, part_y, at_x, near)
                lifted_ref[2, at_x, near : near + 8, :] = walled(2, part_z, at_x, near)
                smoke_ref[at_x, near : near + 8, :] = smoke
            return carry

        lax.fori_loop(start, stop, row, 0)

    rims = (inside[0], inside[-1])
    first_rows(2, block_x - 2, inside[1:-1])
    arrive((2, 3))
    first_rows(2, block_x - 2, rims)
    arrive((0, 1))
    first_rows(0, 2)
    first_rows(block_x - 2, block_x)
    depart(range(4, 12))
    second_rows(2, block_x - 2, inside[1:-1])
    arrive((10, 11))
    second_rows(2, block_x - 2, rims)
    arrive(range(4, 10))
    for at_y in inside:
        (value,) = second(-1, at_y, (0,))
        face_x[0, at_y - low_y : at_y - low_y + 8, :] = walled(0, value, -1, 0)
    second_rows(0, 2)
    second_rows(block_x - 2, block_x)

    def differ(at_x, carry):
        part_x = face_x[at_x + 1]
        part_y = face_y[at_x, 8 : 8 + block_y, :]
        part_z = lifted_ref[2, at_x]
        below = jnp.where(
            lax.broadcasted_iota(jnp.int32, part_z.shape, 1) > 0, pltpu.roll(part_z, 1, 1), 0.0
        )
        lifted_ref[0, at_x] = part_x
        lifted_ref[1, at_x] = part_y
        div_ref[at_x] = (
            part_x
            - face_x[at_x]
            + (part_y - face_y[at_x, 7 : 7 + block_y, :])
            + (part_z - below)
        )
        return carry

    lax.fori_loop(0, block_x, differ, 0)
    for index, move in enumerate(moves):

        @pl.when(exists(move[0], move[1]))
        def _():
            copy_of(index).wait_send()


def halves(value):
    big = value.astype(jnp.bfloat16)
    return big, (value - big.astype(jnp.float32)).astype(jnp.bfloat16)


def dot_split(left, right):
    left_big, left_rest = halves(left)
    right_big, right_rest = halves(right)

    def dot(one, two):
        return jnp.dot(one, two, preferred_element_type=jnp.float32)

    return dot(left_big, right_big) + (dot(left_big, right_rest) + dot(left_rest, right_big))


def dot_full(left, right):
    return jnp.dot(left, right, precision=highest, preferred_element_type=jnp.float32)


def mode_tables(full_x, length_z, slab, groups, anchor_kz):
    modes_x = jnp.arange(full_x, dtype=jnp.float32)[:, None]
    modes_z = (anchor_kz + jnp.arange(slab * groups) % slab).astype(jnp.float32)[None, :]
    shift = 4.0 * (
        jnp.sin(modes_x * (np.pi / (2 * full_x))) ** 2
        + jnp.sin(modes_z * (np.pi / (2 * length_z))) ** 2
    )
    root = jnp.sqrt(shift + 0.25 * shift * shift)
    decay = 1.0 / (1.0 + 0.5 * shift + root)
    zero = (modes_x == 0) & (modes_z == 0)
    gain = jnp.where(zero, 0.0, -0.5 / jnp.where(zero, 1.0, root))
    return decay, gain


def solve_part(
    count_x,
    count_y,
    div_ref,
    lifted_ref,
    total_ref,
    tz_ref,
    tzt_ref,
    tx_ref,
    txt_ref,
    decay_ref,
    gain_ref,
    out_ref,
    emission_ref,
    smoke_ref,
    send_a,
    recv_a,
    send_b,
    recv_b,
    send_e,
    recv_e,
    edge,
    totals,
    sums,
    hat,
    sems_x,
    sems_y,
):
    block_x, block_y, length_z = div_ref.shape
    full_x = block_x * count_x
    me_x = lax.axis_index("gx")
    me_y = lax.axis_index("gy")
    slab = length_z // count_x
    lanes = recv_a.shape[-1]
    groups = lanes // slab
    rows = block_y // groups

    half = rows // 2
    chunks = ((0, half), (half, rows))

    def to_x(kind, source, target, start=None, stop=None):
        copies = []
        for offset in range(1, count_x):
            to = lax.rem(me_x + offset, count_x)
            if source is total_ref:
                source_at, target_at = source, target.at[me_x]
            elif start is None:
                source_at, target_at = source.at[to], target.at[me_x]
            else:
                source_at = source.at[to, pl.ds(start, stop - start)]
                target_at = target.at[me_x, pl.ds(start, stop - start)]
            copies.append(
                pltpu.make_async_remote_copy(
                    src_ref=source_at,
                    dst_ref=target_at,
                    send_sem=sems_x.at[kind, 0, offset],
                    recv_sem=sems_x.at[kind, 1, offset],
                    device_id={"gx": to},
                    device_id_type=pl.DeviceIdType.MESH,
                )
            )
        for copy in copies:
            copy.start()
        return copies

    table = tzt_ref[...]
    copies_a = []
    for kind, (start, stop) in enumerate(chunks):
        size = stop - start
        div = jnp.concatenate(
            [
                jnp.swapaxes(div_ref[:, group * rows + start : group * rows + stop, :], 0, 1)
                for group in range(groups)
            ],
            axis=0,
        )
        along = dot_split(div.reshape(groups * size * block_x, length_z), table)
        along = along.reshape(groups, size, block_x, length_z)
        for target in range(count_x):
            send_a[target, start:stop] = jnp.concatenate(
                [
                    along[group, :, :, target * slab : (target + 1) * slab]
                    for group in range(groups)
                ],
                axis=-1,
            )
        copies_a.append(to_x(kind, send_a, recv_a, start, stop))
    copies_t = to_x(2, total_ref, totals)
    recv_a[me_x] = send_a[me_x]

    lane = lax.broadcasted_iota(jnp.int32, (full_x, lanes), 1)
    group_of = lane // slab
    decay = decay_ref[...]
    gain = gain_ref[...]
    zero = gain == 0.0

    def power(base, count):
        result = None
        while count:
            if count & 1:
                result = base if result is None else result * base
            count >>= 1
            if count:
                base = base * base
        return result

    def up(value):
        return pltpu.roll(value, slab, 1)

    def down(value):
        return pltpu.roll(value, lanes - slab, 1)

    decay_rows = power(decay, rows)
    decay_block = power(decay_rows, groups)
    decay_full = power(decay_block, count_y)

    for copies, (start, stop) in zip(copies_a, chunks):
        for copy in copies:
            copy.wait()
        gathered = jnp.concatenate(
            [
                jnp.concatenate([recv_a[place, row] for place in range(count_x)], axis=0)
                for row in range(start, stop)
            ],
            axis=1,
        )
        modes = dot_split(tx_ref[...], gathered)
        for row in range(start, stop):
            hat[row] = modes[:, (row - start) * lanes : (row - start + 1) * lanes]

    forward = hat[0]
    for row in range(1, rows):
        forward = decay * forward + hat[row]
    backward = hat[rows - 1]
    for row in range(rows - 2, -1, -1):
        backward = decay * backward + hat[row]
    forward_block = forward
    for group in range(1, groups):
        forward_block = jnp.where(
            group_of == group, forward + decay_rows * up(forward_block), forward_block
        )
    backward_block = backward
    for group in range(groups - 2, -1, -1):
        backward_block = jnp.where(
            group_of == group, backward + decay_rows * down(backward_block), backward_block
        )
    sums[me_y] = jnp.where(group_of == 0, backward_block, forward_block)
    copies_s = []
    for offset in range(1, count_y):
        copies_s.append(
            pltpu.make_async_remote_copy(
                src_ref=sums.at[me_y],
                dst_ref=sums.at[me_y],
                send_sem=sems_y.at[0, offset],
                recv_sem=sems_y.at[1, offset],
                device_id={"gy": lax.rem(me_y + offset, count_y)},
                device_id_type=pl.DeviceIdType.MESH,
            )
        )
    for copy in copies_s:
        copy.start()
    for copy in copies_s:
        copy.wait()

    from_low = jnp.zeros_like(decay)
    all_low = jnp.zeros_like(decay)
    power_low = jnp.ones_like(decay)
    from_high = jnp.zeros_like(decay)
    all_high = jnp.zeros_like(decay)
    power_high = jnp.ones_like(decay)
    for place in range(count_y):
        part = sums[place]
        all_low = all_low * decay_block + part
        from_low = jnp.where(place < me_y, from_low * decay_block + part, from_low)
        power_low = jnp.where(place < me_y, power_low * decay_block, power_low)
        other = count_y - 1 - place
        part = sums[other]
        all_high = all_high * decay_block + part
        from_high = jnp.where(other > me_y, from_high * decay_block + part, from_high)
        power_high = jnp.where(other > me_y, power_high * decay_block, power_high)
    first = group_of == 0

    def swap(value):
        return up(value) if groups == 2 else jnp.where(first, up(value), down(value))

    whole = jnp.where(first, all_high, all_low)
    image = jnp.where(
        zero,
        0.0,
        (whole + decay_full * swap(whole)) / jnp.where(zero, 1.0, 1.0 - decay_full * decay_full),
    )
    entering = jnp.where(first, from_high, from_low) + jnp.where(
        first, power_high, power_low
    ) * swap(image)
    carry_up = up(entering)
    for group in range(1, groups):
        carry_up = jnp.where(group_of == group, up(forward + decay_rows * carry_up), carry_up)
    carry_down = down(entering)
    for group in range(groups - 2, -1, -1):
        carry_down = jnp.where(
            group_of == group, down(backward + decay_rows * carry_down), carry_down
        )

    top = slice(0, 8)
    mean = jnp.where(first, whole, up(whole))
    for group in range(2, groups):
        mean = jnp.where(group_of == group, up(mean), mean)
    mean = mean[top] * (1.0 / (block_y * count_y))
    flat = jnp.zeros_like(mean)
    flats = [flat]
    position = (me_y * block_y + group_of[top] * rows).astype(jnp.float32)
    ahead = carry_up
    left = [ahead]
    for row in range(rows):
        ahead = decay * ahead + hat[row]
        left.append(ahead)
        flat = flat + (ahead[top] - (position + (row + 1.0)) * mean)
        flats.append(flat)
    offset_flat = jnp.zeros_like(mean)
    for group in range(1, groups):
        offset_flat = jnp.where(
            group_of[top] == group, up(offset_flat + flats[rows]), offset_flat
        )
    behind = carry_down
    pressures = [None] * (rows + 1)
    for row in range(rows, -1, -1):
        if row < rows:
            behind = decay * behind + hat[row]
        pressure = gain * (decay * left[row] + behind)
        special = jnp.where(zero[top], flats[row] + offset_flat, pressure[top])
        pressures[row] = jnp.concatenate([special, pressure[8:]], axis=0)
    back = dot_full(txt_ref[...], jnp.concatenate(pressures, axis=1))
    for target in range(count_x):
        for row in range(rows + 1):
            columns = slice(row * lanes, (row + 1) * lanes)
            send_b[target, row] = back[target * block_x : (target + 1) * block_x, columns]
            if target < count_x - 1:
                after = (target + 1) * block_x
                send_e[target, row : row + 1, :] = back[after : after + 1, columns]
        if target == count_x - 1:
            send_e[target] = jnp.zeros(send_e.shape[1:], jnp.float32)
    copies_e = to_x(3, send_e, recv_e)
    copies_high = to_x(4, send_b, recv_b, half, rows + 1)
    copies_low = to_x(5, send_b, recv_b, 0, half)
    recv_b[me_x] = send_b[me_x]
    recv_e[me_x] = send_e[me_x]
    for copy in copies_t:
        copy.wait()
    running = jnp.zeros_like(total_ref)
    for place in range(count_x - 1):
        running = jnp.where(place < me_x, running + totals[place], running)
    attenuation = extinction / full_x
    for at_x in range(block_x):
        column = smoke_ref[at_x]
        thickness = attenuation * column
        absorbed = jnp.tanh(0.5 * thickness) * (1.0 + jnp.exp(-thickness))
        emission_ref[at_x] = jnp.exp(-attenuation * running) * absorbed * (1.0 / attenuation)
        running = running + column

    table_back = tz_ref[...]
    for copy in copies_e:
        copy.wait()
    for group in range(groups):
        size = rows + (group == groups - 1)
        edge[group * rows : group * rows + size, :] = jnp.concatenate(
            [
                recv_e[place][:size, group * slab : (group + 1) * slab]
                for place in range(count_x)
            ],
            axis=-1,
        )
    following = dot_full(edge[...], table_back)[:block_y]
    after = None
    for copies, (start, stop) in ((copies_high, (half, rows + 1)), (copies_low, (0, half))):
        for copy in copies:
            copy.wait()
        size = stop - start
        field = jnp.concatenate(
            [
                jnp.concatenate(
                    [
                        recv_b[place, start:stop][..., group * slab : (group + 1) * slab]
                        for place in range(count_x)
                    ],
                    axis=-1,
                )
                for group in range(groups)
            ],
            axis=0,
        )
        field = dot_full(field.reshape(groups * size * block_x, length_z), table_back)
        field = field.reshape(groups, size, block_x, length_z)
        if after is not None:
            field = jnp.concatenate([field, after], axis=1)
        after = field[:, :1]
        for group in range(groups):
            middle = field[group, :half]
            at_y = group * rows + start
            shape = middle.shape
            last_x = lax.broadcasted_iota(jnp.int32, shape, 1) == block_x - 1
            ahead_x = jnp.where(
                last_x, following[at_y : at_y + half][:, None, :], jnp.roll(middle, -1, axis=1)
            )
            ahead_z = pltpu.roll(middle, length_z - 1, 2)
            gradients = (ahead_x - middle, field[group, 1 : half + 1] - middle, ahead_z - middle)
            shape = (block_x, half, length_z)
            opened = (
                lax.broadcasted_iota(jnp.int32, shape, 0) + me_x * block_x < full_x - 1,
                lax.broadcasted_iota(jnp.int32, shape, 1) + (me_y * block_y + at_y)
                < block_y * count_y - 1,
                lax.broadcasted_iota(jnp.int32, shape, 2) < length_z - 1,
            )
            for axis_id in range(3):
                value = lifted_ref[axis_id, :, at_y : at_y + half, :] - jnp.swapaxes(
                    gradients[axis_id], 0, 1
                )
                out_ref[axis_id, :, at_y : at_y + half, :] = jnp.where(
                    opened[axis_id], value, 0.0
                )


def step_kernel(
    count_x,
    count_y,
    velocity_ref,
    density_ref,
    tz_ref,
    tzt_ref,
    tx_ref,
    txt_ref,
    decay_ref,
    gain_ref,
    out_ref,
    emission_ref,
    wide,
    middle,
    face_x,
    face_y,
    sent,
    received,
    lifted,
    smoke,
    div,
    total,
    *rest,
):
    me_x = lax.axis_index("gx")
    me_y = lax.axis_index("gy")
    barrier = pltpu.get_barrier_semaphore()

    def greet(to_x, to_y):
        pl.semaphore_signal(
            barrier,
            inc=1,
            device_id={"gx": to_x, "gy": to_y},
            device_id_type=pl.DeviceIdType.MESH,
        )

    for offset in range(1, count_x):
        greet(lax.rem(me_x + offset, count_x), me_y)
    for offset in range(1, count_y):
        greet(me_x, lax.rem(me_y + offset, count_y))
    for offset_x in (-1, 1):
        for offset_y in (-1, 1):
            to_x = me_x + offset_x
            to_y = me_y + offset_y

            @pl.when((to_x >= 0) & (to_x < count_x) & (to_y >= 0) & (to_y < count_y))
            def _():
                greet(to_x, to_y)

    def meet():
        beside_x = 2 - (me_x == 0).astype(jnp.int32) - (me_x == count_x - 1).astype(jnp.int32)
        beside_y = 2 - (me_y == 0).astype(jnp.int32) - (me_y == count_y - 1).astype(jnp.int32)
        pl.semaphore_wait(barrier, count_x + count_y - 2 + beside_x * beside_y)

    advect_part(
        count_x,
        count_y,
        meet,
        velocity_ref,
        density_ref,
        lifted,
        smoke,
        div,
        wide,
        middle,
        face_x,
        face_y,
        sent,
        received,
    )
    total[...] = jnp.sum(smoke[...], axis=0)
    solve_part(
        count_x,
        count_y,
        div,
        lifted,
        total,
        tz_ref,
        tzt_ref,
        tx_ref,
        txt_ref,
        decay_ref,
        gain_ref,
        out_ref,
        emission_ref,
        smoke,
        *rest,
    )


def per_device(velocity, density):
    block_x, block_y, length_z = density.shape
    count_x = lax.axis_size("gx")
    count_y = lax.axis_size("gy")
    full_x = block_x * count_x
    slab = length_z // count_x
    lanes = 128
    groups = lanes // slab
    rows = block_y // groups
    padded = -(-(rows + 1) // 8) * 8
    table_z = cosine_table(length_z)
    table_x = cosine_table(full_x)
    decay, gain = mode_tables(full_x, length_z, slab, groups, lax.axis_index("gx") * slab)
    vmem = pl.BlockSpec(memory_space=pltpu.VMEM)

    def buffer(*shape):
        return pltpu.VMEM(shape, jnp.float32)

    return pl.pallas_call(
        functools.partial(step_kernel, count_x, count_y),
        out_shape=(
            jax.ShapeDtypeStruct(velocity.shape, jnp.float32),
            jax.ShapeDtypeStruct(density.shape, jnp.float32),
        ),
        in_specs=[vmem] * 8,
        out_specs=(vmem, vmem),
        scratch_shapes=[
            buffer(4, block_x + 4, block_y + 32, length_z),
            buffer(4, block_x + 5, block_y + 32, length_z),
            buffer(block_x + 1, block_y, length_z),
            buffer(block_x, block_y + 8, length_z),
            pltpu.SemaphoreType.DMA((12,)),
            pltpu.SemaphoreType.DMA((12,)),
            buffer(3, block_x, block_y, length_z),
            buffer(block_x, block_y, length_z),
            buffer(block_x, block_y, length_z),
            buffer(block_y, length_z),
            buffer(count_x, rows, block_x, lanes),
            buffer(count_x, rows, block_x, lanes),
            buffer(count_x, rows + 1, block_x, lanes),
            buffer(count_x, rows + 1, block_x, lanes),
            buffer(count_x, padded, lanes),
            buffer(count_x, padded, lanes),
            buffer(block_y + 8, length_z),
            buffer(count_x, block_y, length_z),
            buffer(count_y, full_x, lanes),
            buffer(rows, full_x, lanes),
            pltpu.SemaphoreType.DMA((6, 2, count_x)),
            pltpu.SemaphoreType.DMA((2, count_y)),
        ],
        compiler_params=pltpu.CompilerParams(
            collective_id=0, has_side_effects=True, vmem_limit_bytes=48 * 1024 * 1024
        ),
    )(
        velocity,
        density,
        jnp.asarray(table_z),
        jnp.asarray(table_z.T.copy()),
        jnp.asarray(table_x),
        jnp.asarray(table_x.T.copy()),
        decay,
        gain,
    )


def solution(mesh):
    in_specs = (P(None, "gx", "gy", None), P("gx", "gy", None))
    out_specs = (P(None, "gx", "gy", None), P("gx", "gy", None))
    return jax.shard_map(
        per_device, mesh=mesh, in_specs=in_specs, out_specs=out_specs, check_vma=False
    )
```

```python
import functools

import jax
import jax.numpy as jnp
from jax import lax
from jax.experimental import pallas as pl
from jax.experimental.pallas import tpu as pltpu
from jax.sharding import PartitionSpec as P
import numpy as np

time_step = 0.4
buoyancy = 2.0
extinction = 3.0
highest = lax.Precision.HIGHEST


def cosine_table(length):
    modes = np.arange(length)[:, None]
    centres = np.arange(length)[None, :] + 0.5
    factor = np.where(modes == 0, np.sqrt(1.0 / length), np.sqrt(2.0 / length))
    return (factor * np.cos(np.pi * modes * centres / length)).astype(np.float32)


def advect_part(
    count_x,
    count_y,
    meet,
    velocity_ref,
    density_ref,
    lifted_ref,
    smoke_ref,
    div_ref,
    wide,
    middle,
    face_x,
    face_y,
    sent,
    received,
):
    block_x, block_y, length_z = density_ref.shape
    me_x = lax.axis_index("gx")
    me_y = lax.axis_index("gy")
    last_x = block_x * count_x - 1
    last_y = block_y * count_y - 1
    low_y, high_y, rim = 16, 16 + block_y, 8
    half = block_y // 2
    parts = tuple((start, start, half) for start in (low_y, low_y + half))
    upward = (high_y - rim, low_y - rim, rim)
    downward = (low_y, high_y, rim)
    first_x = [
        [(1, 0, (0, 4), (block_x, 0, 2), part), (-1, 0, (0, 4), (2, block_x + 2, 2), part)]
        for part in parts
    ]
    first_y = [
        (0, 1, (0, 4), (2, 2, block_x), upward),
        (0, -1, (0, 4), (2, 2, block_x), downward),
    ]
    second_x = [
        [
            (1, 0, (0, 4), (block_x + 1, 1, 2), part),
            (-1, 0, (0, 4), (3, block_x + 3, 2), part),
            (1, 0, (0, 1), (block_x, 0, 1), part),
        ]
        for part in parts
    ]
    second_x[0].append((1, -1, (0, 1), (block_x + 2, 2, 1), downward))
    second_x[1].append((1, 1, (0, 2), (block_x + 1, 1, 2), upward))
    second_x[1].append((-1, 1, (1, 1), (3, block_x + 3, 2), upward))
    second_y = [
        (0, 1, (0, 4), (3, 3, block_x), upward),
        (0, -1, (0, 4), (3, 3, block_x), downward),
    ]
    groups = (first_x[0], first_y, first_x[1], second_x[0], second_x[1], second_y)
    moves = [move for group in groups for move in group]
    spans = []
    for group in groups:
        begin = spans[-1].stop if spans else 0
        spans.append(range(begin, begin + len(group)))

    def array_of(index):
        return wide if index < spans[3].start else middle

    def exists(offset_x, offset_y):
        to_x = me_x + offset_x
        to_y = me_y + offset_y
        return (to_x >= 0) & (to_x < count_x) & (to_y >= 0) & (to_y < count_y)

    def copy_of(index):
        offset_x, offset_y, fields, along_x, along_y = moves[index]
        return pltpu.make_async_remote_copy(
            src_ref=array_of(index).at[
                pl.ds(*fields), pl.ds(along_x[0], along_x[2]), pl.ds(along_y[0], along_y[2])
            ],
            dst_ref=array_of(index).at[
                pl.ds(*fields), pl.ds(along_x[1], along_x[2]), pl.ds(along_y[1], along_y[2])
            ],
            send_sem=sent.at[index],
            recv_sem=received.at[index],
            device_id={"gx": me_x + offset_x, "gy": me_y + offset_y},
            device_id_type=pl.DeviceIdType.MESH,
        )

    for field in range(3):
        wide[field, 2 : 2 + block_x, low_y:high_y, :] = velocity_ref[field].astype(jnp.float32)
    wide[3, 2 : 2 + block_x, low_y:high_y, :] = density_ref[...].astype(jnp.float32)
    meet()

    def depart(indices):
        for index in indices:

            @pl.when(exists(moves[index][0], moves[index][1]))
            def _():
                copy_of(index).start()

    depart(range(spans[3].start))
    for index, move in enumerate(moves):
        fields, along_x, along_y = move[2:]

        @pl.when(jnp.logical_not(exists(-move[0], -move[1])))
        def _():
            shape = (fields[1], along_x[2], along_y[2], length_z)
            array_of(index)[
                fields[0] : fields[0] + fields[1],
                along_x[1] : along_x[1] + along_x[2],
                along_y[1] : along_y[1] + along_y[2],
                :,
            ] = jnp.zeros(shape, jnp.float32)

    def arrive(indices):
        for index in indices:

            @pl.when(exists(-moves[index][0], -moves[index][1]))
            def _():
                copy_of(index).wait_recv()

    lane = lax.broadcasted_iota(jnp.int32, (8, length_z), 1)
    line = lax.broadcasted_iota(jnp.int32, (8, length_z), 0)
    scale = -time_step / 12.0

    def advance(source, at_x, at_y, fields):
        centres = [source[field, at_x, at_y : at_y + 8, :] for field in range(4)]
        weights = []
        base = None
        for axis_id in range(3):
            speed = scale * centres[axis_id]
            size = jnp.abs(speed)
            eight = 8.0 * speed
            four = 4.0 * size
            parts = {1: four + eight, -1: four - eight, 2: -speed - size, -2: speed - size}
            if axis_id == 2:
                parts[1] = jnp.where(lane < length_z - 1, parts[1], 0.0)
                parts[2] = jnp.where(lane < length_z - 2, parts[2], 0.0)
                parts[-1] = jnp.where(lane > 0, parts[-1], 0.0)
                parts[-2] = jnp.where(lane > 1, parts[-2], 0.0)
            weights.append(parts)
            base = size if base is None else base + size
        base = 1.0 - 6.0 * base
        results = []
        for field in fields:
            total = centres[field] * base
            for offset in (-2, -1, 1, 2):
                total = total + weights[0][offset] * source[
                    field, at_x + offset, at_y : at_y + 8, :
                ]
                total = total + weights[1][offset] * source[
                    field, at_x, at_y + offset : at_y + offset + 8, :
                ]
                total = total + weights[2][offset] * pltpu.roll(
                    centres[field], (-offset) % length_z, 1
                )
            results.append(total)
        return results

    def walled(field, value, at_x, at_y):
        if field == 0:
            return value * jnp.where(me_x * block_x + at_x == last_x, 0.0, 1.0)
        if field == 1:
            return jnp.where(me_y * block_y + at_y + line == last_y, 0.0, value)
        if field == 2:
            return jnp.where(lane == length_z - 1, 0.0, value)
        return value

    inside = tuple(range(low_y, high_y, 8))

    def first_rows(start, stop, tiles=inside):
        def row(at_x, carry):
            for at_y in tiles:
                values = advance(wide, at_x + 2, at_y, (0, 1, 2, 3))
                for field, value in enumerate(values):
                    middle[field, at_x + 3, at_y : at_y + 8, :] = walled(
                        field, value, at_x, at_y - low_y
                    )
            return carry

        lax.fori_loop(start, stop, row, 0)

    def second(at_x, at_y, fields):
        values = advance(middle, at_x + 3, at_y, fields)
        return [
            0.5 * wide[field, at_x + 2, at_y : at_y + 8, :] + 0.5 * value
            for field, value in zip(fields, values)
        ]

    def second_rows(start, stop, tiles=inside):
        def row(at_x, carry):
            if inside[0] in tiles:
                (value,) = second(at_x, low_y - 8, (1,))
                face_y[at_x, 0:8, :] = walled(1, value, at_x, -8)
            for at_y in tiles:
                near = at_y - low_y
                part_x, part_y, part_z, smoke = second(at_x, at_y, (0, 1, 2, 3))
                above = pltpu.roll(smoke, length_z - 1, 1)
                part_z = part_z + (time_step * buoyancy * 0.5) * (smoke + above)
                face_x[at_x + 1, near : near + 8, :] = walled(0, part_x, at_x, near)
                face_y[at_x, near + 8 : near + 16, :] = walled(1, part_y, at_x, near)
                lifted_ref[2, at_x, near : near + 8, :] = walled(2, part_z, at_x, near)
                smoke_ref[at_x, near : near + 8, :] = smoke
            return carry

        lax.fori_loop(start, stop, row, 0)

    rims = (inside[0], inside[-1])
    first_rows(2, block_x - 2, inside[1:-1])
    arrive(spans[1])
    first_rows(2, block_x - 2, rims)
    for part in range(2):
        lines = inside[part * len(inside) // 2 : (part + 1) * len(inside) // 2]
        arrive(spans[2 * part])
        first_rows(0, 2, lines)
        first_rows(block_x - 2, block_x, lines)
        depart(spans[3 + part])
    depart(spans[5])
    second_rows(2, block_x - 2, inside[1:-1])
    arrive(spans[5])
    second_rows(2, block_x - 2, rims)
    arrive([*spans[3], *spans[4]])
    for at_y in inside:
        (value,) = second(-1, at_y, (0,))
        face_x[0, at_y - low_y : at_y - low_y + 8, :] = walled(0, value, -1, 0)
    second_rows(0, 2)
    second_rows(block_x - 2, block_x)

    def differ(at_x, carry):
        part_x = face_x[at_x + 1]
        part_y = face_y[at_x, 8 : 8 + block_y, :]
        part_z = lifted_ref[2, at_x]
        below = jnp.where(
            lax.broadcasted_iota(jnp.int32, part_z.shape, 1) > 0, pltpu.roll(part_z, 1, 1), 0.0
        )
        lifted_ref[0, at_x] = part_x
        lifted_ref[1, at_x] = part_y
        div_ref[at_x] = (
            part_x
            - face_x[at_x]
            + (part_y - face_y[at_x, 7 : 7 + block_y, :])
            + (part_z - below)
        )
        return carry

    lax.fori_loop(0, block_x, differ, 0)
    for index, move in enumerate(moves):

        @pl.when(exists(move[0], move[1]))
        def _():
            copy_of(index).wait_send()


def halves(value):
    big = value.astype(jnp.bfloat16)
    return big, (value - big.astype(jnp.float32)).astype(jnp.bfloat16)


def dot_split(left, right):
    left_big, left_rest = halves(left)
    right_big, right_rest = halves(right)

    def dot(one, two):
        return jnp.dot(one, two, preferred_element_type=jnp.float32)

    return dot(left_big, right_big) + (dot(left_big, right_rest) + dot(left_rest, right_big))


def dot_full(left, right):
    return jnp.dot(left, right, precision=highest, preferred_element_type=jnp.float32)


def mode_tables(full_x, length_z, slab, groups, anchor_kz):
    modes_x = jnp.arange(full_x, dtype=jnp.float32)[:, None]
    modes_z = (anchor_kz + jnp.arange(slab * groups) % slab).astype(jnp.float32)[None, :]
    shift = 4.0 * (
        jnp.sin(modes_x * (np.pi / (2 * full_x))) ** 2
        + jnp.sin(modes_z * (np.pi / (2 * length_z))) ** 2
    )
    root = jnp.sqrt(shift + 0.25 * shift * shift)
    decay = 1.0 / (1.0 + 0.5 * shift + root)
    zero = (modes_x == 0) & (modes_z == 0)
    gain = jnp.where(zero, 0.0, -0.5 / jnp.where(zero, 1.0, root))
    return decay, gain


def solve_part(
    count_x,
    count_y,
    div_ref,
    lifted_ref,
    total_ref,
    tz_ref,
    tzt_ref,
    tx_ref,
    txt_ref,
    decay_ref,
    gain_ref,
    out_ref,
    emission_ref,
    smoke_ref,
    send_a,
    recv_a,
    send_b,
    recv_b,
    send_e,
    recv_e,
    edge,
    totals,
    sums,
    hat,
    sems_x,
    sems_y,
):
    block_x, block_y, length_z = div_ref.shape
    full_x = block_x * count_x
    me_x = lax.axis_index("gx")
    me_y = lax.axis_index("gy")
    slab = length_z // count_x
    lanes = recv_a.shape[-1]
    groups = lanes // slab
    rows = block_y // groups

    half = rows // 2
    chunks = ((0, half), (half, rows))

    def to_x(kind, source, target, start=None, stop=None):
        copies = []
        for offset in range(1, count_x):
            to = lax.rem(me_x + offset, count_x)
            if source is total_ref:
                source_at, target_at = source, target.at[me_x]
            elif start is None:
                source_at, target_at = source.at[to], target.at[me_x]
            else:
                source_at = source.at[to, pl.ds(start, stop - start)]
                target_at = target.at[me_x, pl.ds(start, stop - start)]
            copies.append(
                pltpu.make_async_remote_copy(
                    src_ref=source_at,
                    dst_ref=target_at,
                    send_sem=sems_x.at[kind, 0, offset],
                    recv_sem=sems_x.at[kind, 1, offset],
                    device_id={"gx": to},
                    device_id_type=pl.DeviceIdType.MESH,
                )
            )
        for copy in copies:
            copy.start()
        return copies

    table = tzt_ref[...]
    copies_a = []
    for kind, (start, stop) in enumerate(chunks):
        size = stop - start
        div = jnp.concatenate(
            [
                jnp.swapaxes(div_ref[:, group * rows + start : group * rows + stop, :], 0, 1)
                for group in range(groups)
            ],
            axis=0,
        )
        along = dot_split(div.reshape(groups * size * block_x, length_z), table)
        along = along.reshape(groups, size, block_x, length_z)
        for target in range(count_x):
            send_a[target, start:stop] = jnp.concatenate(
                [
                    along[group, :, :, target * slab : (target + 1) * slab]
                    for group in range(groups)
                ],
                axis=-1,
            )
        copies_a.append(to_x(kind, send_a, recv_a, start, stop))
    copies_t = to_x(2, total_ref, totals)
    recv_a[me_x] = send_a[me_x]

    lane = lax.broadcasted_iota(jnp.int32, (full_x, lanes), 1)
    group_of = lane // slab
    decay = decay_ref[...]
    gain = gain_ref[...]
    zero = gain == 0.0

    def power(base, count):
        result = None
        while count:
            if count & 1:
                result = base if result is None else result * base
            count >>= 1
            if count:
                base = base * base
        return result

    def up(value):
        return pltpu.roll(value, slab, 1)

    def down(value):
        return pltpu.roll(value, lanes - slab, 1)

    decay_rows = power(decay, rows)
    decay_block = power(decay_rows, groups)
    decay_full = power(decay_block, count_y)

    for copies, (start, stop) in zip(copies_a, chunks):
        for copy in copies:
            copy.wait()
        gathered = jnp.concatenate(
            [
                jnp.concatenate([recv_a[place, row] for place in range(count_x)], axis=0)
                for row in range(start, stop)
            ],
            axis=1,
        )
        modes = dot_split(tx_ref[...], gathered)
        for row in range(start, stop):
            hat[row] = modes[:, (row - start) * lanes : (row - start + 1) * lanes]

    forward = hat[0]
    for row in range(1, rows):
        forward = decay * forward + hat[row]
    backward = hat[rows - 1]
    for row in range(rows - 2, -1, -1):
        backward = decay * backward + hat[row]
    forward_block = forward
    for group in range(1, groups):
        forward_block = jnp.where(
            group_of == group, forward + decay_rows * up(forward_block), forward_block
        )
    backward_block = backward
    for group in range(groups - 2, -1, -1):
        backward_block = jnp.where(
            group_of == group, backward + decay_rows * down(backward_block), backward_block
        )
    sums[me_y] = jnp.where(group_of == 0, backward_block, forward_block)
    copies_s = []
    for offset in range(1, count_y):
        copies_s.append(
            pltpu.make_async_remote_copy(
                src_ref=sums.at[me_y],
                dst_ref=sums.at[me_y],
                send_sem=sems_y.at[0, offset],
                recv_sem=sems_y.at[1, offset],
                device_id={"gy": lax.rem(me_y + offset, count_y)},
                device_id_type=pl.DeviceIdType.MESH,
            )
        )
    for copy in copies_s:
        copy.start()
    for copy in copies_s:
        copy.wait()

    from_low = jnp.zeros_like(decay)
    all_low = jnp.zeros_like(decay)
    power_low = jnp.ones_like(decay)
    from_high = jnp.zeros_like(decay)
    all_high = jnp.zeros_like(decay)
    power_high = jnp.ones_like(decay)
    for place in range(count_y):
        part = sums[place]
        all_low = all_low * decay_block + part
        from_low = jnp.where(place < me_y, from_low * decay_block + part, from_low)
        power_low = jnp.where(place < me_y, power_low * decay_block, power_low)
        other = count_y - 1 - place
        part = sums[other]
        all_high = all_high * decay_block + part
        from_high = jnp.where(other > me_y, from_high * decay_block + part, from_high)
        power_high = jnp.where(other > me_y, power_high * decay_block, power_high)
    first = group_of == 0

    def swap(value):
        return up(value) if groups == 2 else jnp.where(first, up(value), down(value))

    whole = jnp.where(first, all_high, all_low)
    image = jnp.where(
        zero,
        0.0,
        (whole + decay_full * swap(whole)) / jnp.where(zero, 1.0, 1.0 - decay_full * decay_full),
    )
    entering = jnp.where(first, from_high, from_low) + jnp.where(
        first, power_high, power_low
    ) * swap(image)
    carry_up = up(entering)
    for group in range(1, groups):
        carry_up = jnp.where(group_of == group, up(forward + decay_rows * carry_up), carry_up)
    carry_down = down(entering)
    for group in range(groups - 2, -1, -1):
        carry_down = jnp.where(
            group_of == group, down(backward + decay_rows * carry_down), carry_down
        )

    top = slice(0, 8)
    mean = jnp.where(first, whole, up(whole))
    for group in range(2, groups):
        mean = jnp.where(group_of == group, up(mean), mean)
    mean = mean[top] * (1.0 / (block_y * count_y))
    flat = jnp.zeros_like(mean)
    flats = [flat]
    position = (me_y * block_y + group_of[top] * rows).astype(jnp.float32)
    ahead = carry_up
    left = [ahead]
    for row in range(rows):
        ahead = decay * ahead + hat[row]
        left.append(ahead)
        flat = flat + (ahead[top] - (position + (row + 1.0)) * mean)
        flats.append(flat)
    offset_flat = jnp.zeros_like(mean)
    for group in range(1, groups):
        offset_flat = jnp.where(
            group_of[top] == group, up(offset_flat + flats[rows]), offset_flat
        )
    behind = carry_down
    pressures = [None] * (rows + 1)
    for row in range(rows, -1, -1):
        if row < rows:
            behind = decay * behind + hat[row]
        pressure = gain * (decay * left[row] + behind)
        special = jnp.where(zero[top], flats[row] + offset_flat, pressure[top])
        pressures[row] = jnp.concatenate([special, pressure[8:]], axis=0)
    back = dot_full(txt_ref[...], jnp.concatenate(pressures, axis=1))
    for target in range(count_x):
        for row in range(rows + 1):
            columns = slice(row * lanes, (row + 1) * lanes)
            send_b[target, row] = back[target * block_x : (target + 1) * block_x, columns]
            if target < count_x - 1:
                after = (target + 1) * block_x
                send_e[target, row : row + 1, :] = back[after : after + 1, columns]
        if target == count_x - 1:
            send_e[target] = jnp.zeros(send_e.shape[1:], jnp.float32)
    copies_e = to_x(3, send_e, recv_e)
    copies_high = to_x(4, send_b, recv_b, half, rows + 1)
    copies_low = to_x(5, send_b, recv_b, 0, half)
    recv_b[me_x] = send_b[me_x]
    recv_e[me_x] = send_e[me_x]
    for copy in copies_t:
        copy.wait()
    running = jnp.zeros_like(total_ref)
    for place in range(count_x - 1):
        running = jnp.where(place < me_x, running + totals[place], running)
    attenuation = extinction / full_x
    for at_x in range(block_x):
        column = smoke_ref[at_x]
        thickness = attenuation * column
        absorbed = jnp.tanh(0.5 * thickness) * (1.0 + jnp.exp(-thickness))
        emission_ref[at_x] = jnp.exp(-attenuation * running) * absorbed * (1.0 / attenuation)
        running = running + column

    table_back = tz_ref[...]
    for copy in copies_e:
        copy.wait()
    for group in range(groups):
        size = rows + (group == groups - 1)
        edge[group * rows : group * rows + size, :] = jnp.concatenate(
            [
                recv_e[place][:size, group * slab : (group + 1) * slab]
                for place in range(count_x)
            ],
            axis=-1,
        )
    following = dot_full(edge[...], table_back)[:block_y]
    after = None
    for copies, (start, stop) in ((copies_high, (half, rows + 1)), (copies_low, (0, half))):
        for copy in copies:
            copy.wait()
        size = stop - start
        field = jnp.concatenate(
            [
                jnp.concatenate(
                    [
                        recv_b[place, start:stop][..., group * slab : (group + 1) * slab]
                        for place in range(count_x)
                    ],
                    axis=-1,
                )
                for group in range(groups)
            ],
            axis=0,
        )
        field = dot_full(field.reshape(groups * size * block_x, length_z), table_back)
        field = field.reshape(groups, size, block_x, length_z)
        if after is not None:
            field = jnp.concatenate([field, after], axis=1)
        after = field[:, :1]
        for group in range(groups):
            at_y = group * rows + start
            middle = jnp.swapaxes(field[group, :half], 0, 1)
            ahead_x = jnp.concatenate([middle[1:], following[None, at_y : at_y + half]], axis=0)
            shape = middle.shape
            line = lax.broadcasted_iota(jnp.int32, shape, 1)
            ahead_y = jnp.where(
                line == half - 1, field[group, half][:, None, :], jnp.roll(middle, -1, axis=1)
            )
            ahead_z = pltpu.roll(middle, length_z - 1, 2)
            opened = (
                lax.broadcasted_iota(jnp.int32, shape, 0) + me_x * block_x < full_x - 1,
                line + (me_y * block_y + at_y) < block_y * count_y - 1,
                lax.broadcasted_iota(jnp.int32, shape, 2) < length_z - 1,
            )
            for axis_id, ahead in enumerate((ahead_x, ahead_y, ahead_z)):
                value = lifted_ref[axis_id, :, at_y : at_y + half, :] - (ahead - middle)
                out_ref[axis_id, :, at_y : at_y + half, :] = jnp.where(
                    opened[axis_id], value, 0.0
                )


def step_kernel(
    count_x,
    count_y,
    velocity_ref,
    density_ref,
    tz_ref,
    tzt_ref,
    tx_ref,
    txt_ref,
    decay_ref,
    gain_ref,
    out_ref,
    emission_ref,
    wide,
    middle,
    face_x,
    face_y,
    sent,
    received,
    lifted,
    smoke,
    div,
    total,
    *rest,
):
    me_x = lax.axis_index("gx")
    me_y = lax.axis_index("gy")
    *rest, fetched = rest
    given = (velocity_ref, density_ref, tz_ref, tzt_ref, tx_ref, txt_ref, decay_ref, gain_ref)
    held, rest = rest[-len(given) :], rest[: -len(given)]
    fetches = [
        pltpu.make_async_copy(source, target, fetched.at[index])
        for index, (source, target) in enumerate(zip(given, held))
    ]
    for fetch in fetches:
        fetch.start()
    barrier = pltpu.get_barrier_semaphore()

    def greet(to_x, to_y):
        pl.semaphore_signal(
            barrier,
            inc=1,
            device_id={"gx": to_x, "gy": to_y},
            device_id_type=pl.DeviceIdType.MESH,
        )

    for offset in range(1, count_x):
        greet(lax.rem(me_x + offset, count_x), me_y)
    for offset in range(1, count_y):
        greet(me_x, lax.rem(me_y + offset, count_y))
    for offset_x in (-1, 1):
        for offset_y in (-1, 1):
            to_x = me_x + offset_x
            to_y = me_y + offset_y

            @pl.when((to_x >= 0) & (to_x < count_x) & (to_y >= 0) & (to_y < count_y))
            def _():
                greet(to_x, to_y)

    def meet():
        beside_x = 2 - (me_x == 0).astype(jnp.int32) - (me_x == count_x - 1).astype(jnp.int32)
        beside_y = 2 - (me_y == 0).astype(jnp.int32) - (me_y == count_y - 1).astype(jnp.int32)
        pl.semaphore_wait(barrier, count_x + count_y - 2 + beside_x * beside_y)

    for fetch in fetches[:2]:
        fetch.wait()
    advect_part(
        count_x,
        count_y,
        meet,
        *held[:2],
        lifted,
        smoke,
        div,
        wide,
        middle,
        face_x,
        face_y,
        sent,
        received,
    )
    total[...] = jnp.sum(smoke[...], axis=0)
    for fetch in fetches[2:]:
        fetch.wait()
    solve_part(
        count_x,
        count_y,
        div,
        lifted,
        total,
        *held[2:],
        out_ref,
        emission_ref,
        smoke,
        *rest,
    )


def per_device(velocity, density):
    block_x, block_y, length_z = density.shape
    count_x = lax.axis_size("gx")
    count_y = lax.axis_size("gy")
    full_x = block_x * count_x
    slab = length_z // count_x
    lanes = 128
    groups = lanes // slab
    rows = block_y // groups
    padded = -(-(rows + 1) // 8) * 8
    table_z = cosine_table(length_z)
    table_x = cosine_table(full_x)
    decay, gain = mode_tables(full_x, length_z, slab, groups, lax.axis_index("gx") * slab)
    operands = (
        velocity,
        density,
        jnp.asarray(table_z),
        jnp.asarray(table_z.T.copy()),
        jnp.asarray(table_x),
        jnp.asarray(table_x.T.copy()),
        decay,
        gain,
    )
    vmem = pl.BlockSpec(memory_space=pltpu.VMEM)

    def buffer(*shape):
        return pltpu.VMEM(shape, jnp.float32)

    return pl.pallas_call(
        functools.partial(step_kernel, count_x, count_y),
        out_shape=(
            jax.ShapeDtypeStruct(velocity.shape, jnp.float32),
            jax.ShapeDtypeStruct(density.shape, jnp.float32),
        ),
        in_specs=[pl.BlockSpec(memory_space=pltpu.HBM)] * 8,
        out_specs=(vmem, vmem),
        scratch_shapes=[
            buffer(4, block_x + 4, block_y + 32, length_z),
            buffer(4, block_x + 5, block_y + 32, length_z),
            buffer(block_x + 1, block_y, length_z),
            buffer(block_x, block_y + 8, length_z),
            pltpu.SemaphoreType.DMA((17,)),
            pltpu.SemaphoreType.DMA((17,)),
            buffer(3, block_x, block_y, length_z),
            buffer(block_x, block_y, length_z),
            buffer(block_x, block_y, length_z),
            buffer(block_y, length_z),
            buffer(count_x, rows, block_x, lanes),
            buffer(count_x, rows, block_x, lanes),
            buffer(count_x, rows + 1, block_x, lanes),
            buffer(count_x, rows + 1, block_x, lanes),
            buffer(count_x, padded, lanes),
            buffer(count_x, padded, lanes),
            buffer(block_y + 8, length_z),
            buffer(count_x, block_y, length_z),
            buffer(count_y, full_x, lanes),
            buffer(rows, full_x, lanes),
            pltpu.SemaphoreType.DMA((6, 2, count_x)),
            pltpu.SemaphoreType.DMA((2, count_y)),
            *[pltpu.VMEM(value.shape, value.dtype) for value in operands],
            pltpu.SemaphoreType.DMA((len(operands),)),
        ],
        compiler_params=pltpu.CompilerParams(
            collective_id=0, has_side_effects=True, vmem_limit_bytes=48 * 1024 * 1024
        ),
    )(*operands)


def solution(mesh):
    in_specs = (P(None, "gx", "gy", None), P("gx", "gy", None))
    out_specs = (P(None, "gx", "gy", None), P("gx", "gy", None))
    return jax.shard_map(
        per_device, mesh=mesh, in_specs=in_specs, out_specs=out_specs, check_vma=False
    )
```

```python
import functools

import jax
import jax.numpy as jnp
from jax import lax
from jax.experimental import pallas as pl
from jax.experimental.pallas import tpu as pltpu
from jax.sharding import PartitionSpec as P
import numpy as np

time_step = 0.4
buoyancy = 2.0
extinction = 3.0
highest = lax.Precision.HIGHEST


def cosine_table(length):
    modes = np.arange(length)[:, None]
    centres = np.arange(length)[None, :] + 0.5
    factor = np.where(modes == 0, np.sqrt(1.0 / length), np.sqrt(2.0 / length))
    return (factor * np.cos(np.pi * modes * centres / length)).astype(np.float32)


def advect_part(
    count_x,
    count_y,
    meet,
    velocity_ref,
    density_ref,
    lifted_ref,
    smoke_ref,
    div_ref,
    wide,
    middle,
    face_x,
    face_y,
    sent,
    received,
):
    block_x, block_y, length_z = density_ref.shape
    me_x = lax.axis_index("gx")
    me_y = lax.axis_index("gy")
    last_x = block_x * count_x - 1
    last_y = block_y * count_y - 1
    low_y, high_y, rim = 16, 16 + block_y, 8
    half = block_y // 2
    parts = tuple((start, start, half) for start in (low_y, low_y + half))
    upward = (high_y - rim, low_y - rim, rim)
    downward = (low_y, high_y, rim)
    first_x = [
        [(1, 0, (0, 4), (block_x, 0, 2), part), (-1, 0, (0, 4), (2, block_x + 2, 2), part)]
        for part in parts
    ]
    first_y = [
        (0, 1, (0, 4), (2, 2, block_x), upward),
        (0, -1, (0, 4), (2, 2, block_x), downward),
    ]
    second_x = [
        [
            (1, 0, (0, 4), (block_x + 1, 1, 2), part),
            (-1, 0, (0, 4), (3, block_x + 3, 2), part),
            (1, 0, (0, 1), (block_x, 0, 1), part),
        ]
        for part in parts
    ]
    second_x[0].append((1, -1, (0, 1), (block_x + 2, 2, 1), downward))
    second_x[1].append((1, 1, (0, 2), (block_x + 1, 1, 2), upward))
    second_x[1].append((-1, 1, (1, 1), (3, block_x + 3, 2), upward))
    second_y = [
        (0, 1, (0, 4), (3, 3, block_x), upward),
        (0, -1, (0, 4), (3, 3, block_x), downward),
    ]
    groups = (first_x[0], first_y, first_x[1], second_x[0], second_x[1], second_y)
    moves = [move for group in groups for move in group]
    spans = []
    for group in groups:
        begin = spans[-1].stop if spans else 0
        spans.append(range(begin, begin + len(group)))

    def array_of(index):
        return wide if index < spans[3].start else middle

    def exists(offset_x, offset_y):
        to_x = me_x + offset_x
        to_y = me_y + offset_y
        return (to_x >= 0) & (to_x < count_x) & (to_y >= 0) & (to_y < count_y)

    def copy_of(index):
        offset_x, offset_y, fields, along_x, along_y = moves[index]
        return pltpu.make_async_remote_copy(
            src_ref=array_of(index).at[
                pl.ds(*fields), pl.ds(along_x[0], along_x[2]), pl.ds(along_y[0], along_y[2])
            ],
            dst_ref=array_of(index).at[
                pl.ds(*fields), pl.ds(along_x[1], along_x[2]), pl.ds(along_y[1], along_y[2])
            ],
            send_sem=sent.at[index],
            recv_sem=received.at[index],
            device_id={"gx": me_x + offset_x, "gy": me_y + offset_y},
            device_id_type=pl.DeviceIdType.MESH,
        )

    for field in range(3):
        wide[field, 2 : 2 + block_x, low_y:high_y, :] = velocity_ref[field].astype(jnp.float32)
    wide[3, 2 : 2 + block_x, low_y:high_y, :] = density_ref[...].astype(jnp.float32)
    meet()

    def depart(indices):
        for index in indices:

            @pl.when(exists(moves[index][0], moves[index][1]))
            def _():
                copy_of(index).start()

    depart(range(spans[3].start))
    for index, move in enumerate(moves):
        fields, along_x, along_y = move[2:]

        @pl.when(jnp.logical_not(exists(-move[0], -move[1])))
        def _():
            shape = (fields[1], along_x[2], along_y[2], length_z)
            array_of(index)[
                fields[0] : fields[0] + fields[1],
                along_x[1] : along_x[1] + along_x[2],
                along_y[1] : along_y[1] + along_y[2],
                :,
            ] = jnp.zeros(shape, jnp.float32)

    def arrive(indices):
        for index in indices:

            @pl.when(exists(-moves[index][0], -moves[index][1]))
            def _():
                copy_of(index).wait_recv()

    lane = lax.broadcasted_iota(jnp.int32, (8, length_z), 1)
    line = lax.broadcasted_iota(jnp.int32, (8, length_z), 0)
    scale = -time_step / 12.0

    def advance(source, at_x, at_y, fields):
        centres = [source[field, at_x, at_y : at_y + 8, :] for field in range(4)]
        weights = []
        base = None
        for axis_id in range(3):
            speed = scale * centres[axis_id]
            size = jnp.abs(speed)
            eight = 8.0 * speed
            four = 4.0 * size
            parts = {1: four + eight, -1: four - eight, 2: -speed - size, -2: speed - size}
            if axis_id == 2:
                parts[1] = jnp.where(lane < length_z - 1, parts[1], 0.0)
                parts[2] = jnp.where(lane < length_z - 2, parts[2], 0.0)
                parts[-1] = jnp.where(lane > 0, parts[-1], 0.0)
                parts[-2] = jnp.where(lane > 1, parts[-2], 0.0)
            weights.append(parts)
            base = size if base is None else base + size
        base = 1.0 - 6.0 * base
        results = []
        for field in fields:
            total = centres[field] * base
            for offset in (-2, -1, 1, 2):
                total = total + weights[0][offset] * source[
                    field, at_x + offset, at_y : at_y + 8, :
                ]
                total = total + weights[1][offset] * source[
                    field, at_x, at_y + offset : at_y + offset + 8, :
                ]
                total = total + weights[2][offset] * pltpu.roll(
                    centres[field], (-offset) % length_z, 1
                )
            results.append(total)
        return results

    def walled(field, value, at_x, at_y):
        if field == 0:
            return value * jnp.where(me_x * block_x + at_x == last_x, 0.0, 1.0)
        if field == 1:
            return jnp.where(me_y * block_y + at_y + line == last_y, 0.0, value)
        if field == 2:
            return jnp.where(lane == length_z - 1, 0.0, value)
        return value

    inside = tuple(range(low_y, high_y, 8))

    def first_rows(start, stop, tiles=inside):
        def row(at_x, carry):
            for at_y in tiles:
                values = advance(wide, at_x + 2, at_y, (0, 1, 2, 3))
                for field, value in enumerate(values):
                    middle[field, at_x + 3, at_y : at_y + 8, :] = walled(
                        field, value, at_x, at_y - low_y
                    )
            return carry

        lax.fori_loop(start, stop, row, 0)

    def second(at_x, at_y, fields):
        values = advance(middle, at_x + 3, at_y, fields)
        return [
            0.5 * wide[field, at_x + 2, at_y : at_y + 8, :] + 0.5 * value
            for field, value in zip(fields, values)
        ]

    def second_rows(start, stop, tiles=inside):
        def row(at_x, carry):
            if inside[0] in tiles:
                (value,) = second(at_x, low_y - 8, (1,))
                face_y[at_x, 0:8, :] = walled(1, value, at_x, -8)
            for at_y in tiles:
                near = at_y - low_y
                part_x, part_y, part_z, smoke = second(at_x, at_y, (0, 1, 2, 3))
                above = pltpu.roll(smoke, length_z - 1, 1)
                part_z = part_z + (time_step * buoyancy * 0.5) * (smoke + above)
                face_x[at_x + 1, near : near + 8, :] = walled(0, part_x, at_x, near)
                face_y[at_x, near + 8 : near + 16, :] = walled(1, part_y, at_x, near)
                lifted_ref[2, at_x, near : near + 8, :] = walled(2, part_z, at_x, near)
                smoke_ref[at_x, near : near + 8, :] = smoke
            return carry

        lax.fori_loop(start, stop, row, 0)

    rims = (inside[0], inside[-1])
    first_rows(2, block_x - 2, inside[1:-1])
    arrive(spans[1])
    first_rows(2, block_x - 2, rims)
    for part in range(2):
        lines = inside[part * len(inside) // 2 : (part + 1) * len(inside) // 2]
        arrive(spans[2 * part])
        first_rows(0, 2, lines)
        first_rows(block_x - 2, block_x, lines)
        depart(spans[3 + part])
    depart(spans[5])
    second_rows(2, block_x - 2, inside[1:-1])
    arrive(spans[5])
    second_rows(2, block_x - 2, rims)
    arrive([*spans[3], *spans[4]])
    for at_y in inside:
        (value,) = second(-1, at_y, (0,))
        face_x[0, at_y - low_y : at_y - low_y + 8, :] = walled(0, value, -1, 0)
    second_rows(0, 2)
    second_rows(block_x - 2, block_x)

    def differ(at_x, carry):
        part_x = face_x[at_x + 1]
        part_y = face_y[at_x, 8 : 8 + block_y, :]
        part_z = lifted_ref[2, at_x]
        below = jnp.where(
            lax.broadcasted_iota(jnp.int32, part_z.shape, 1) > 0, pltpu.roll(part_z, 1, 1), 0.0
        )
        lifted_ref[0, at_x] = part_x
        lifted_ref[1, at_x] = part_y
        div_ref[at_x] = (
            part_x
            - face_x[at_x]
            + (part_y - face_y[at_x, 7 : 7 + block_y, :])
            + (part_z - below)
        )
        return carry

    lax.fori_loop(0, block_x, differ, 0)
    for index, move in enumerate(moves):

        @pl.when(exists(move[0], move[1]))
        def _():
            copy_of(index).wait_send()


def halves(value):
    big = value.astype(jnp.bfloat16)
    return big, (value - big.astype(jnp.float32)).astype(jnp.bfloat16)


def dot_split(left, right):
    left_big, left_rest = halves(left)
    right_big, right_rest = halves(right)

    def dot(one, two):
        return jnp.dot(one, two, preferred_element_type=jnp.float32)

    return dot(left_big, right_big) + (dot(left_big, right_rest) + dot(left_rest, right_big))


def dot_full(left, right):
    return jnp.dot(left, right, precision=highest, preferred_element_type=jnp.float32)


def mode_tables(full_x, length_z, slab, groups, anchor_kz):
    modes_x = jnp.arange(full_x, dtype=jnp.float32)[:, None]
    modes_z = (anchor_kz + jnp.arange(slab * groups) % slab).astype(jnp.float32)[None, :]
    shift = 4.0 * (
        jnp.sin(modes_x * (np.pi / (2 * full_x))) ** 2
        + jnp.sin(modes_z * (np.pi / (2 * length_z))) ** 2
    )
    root = jnp.sqrt(shift + 0.25 * shift * shift)
    decay = 1.0 / (1.0 + 0.5 * shift + root)
    zero = (modes_x == 0) & (modes_z == 0)
    gain = jnp.where(zero, 0.0, -0.5 / jnp.where(zero, 1.0, root))
    return decay, gain


def solve_part(
    count_x,
    count_y,
    div_ref,
    lifted_ref,
    total_ref,
    tz_ref,
    tzt_ref,
    tx_ref,
    txt_ref,
    decay_ref,
    gain_ref,
    out_ref,
    emission_ref,
    smoke_ref,
    send_a,
    recv_a,
    send_b,
    recv_b,
    send_e,
    recv_e,
    edge,
    totals,
    sums,
    hat,
    sems_x,
    sems_y,
):
    block_x, block_y, length_z = div_ref.shape
    full_x = block_x * count_x
    me_x = lax.axis_index("gx")
    me_y = lax.axis_index("gy")
    slab = length_z // count_x
    lanes = recv_a.shape[-1]
    groups = lanes // slab
    rows = block_y // groups

    half = rows // 2
    chunks = ((0, half), (half, rows))

    def to_x(kind, source, target, start=None, stop=None):
        copies = []
        for offset in range(1, count_x):
            to = lax.rem(me_x + offset, count_x)
            if source is total_ref:
                source_at, target_at = source, target.at[me_x]
            elif start is None:
                source_at, target_at = source.at[to], target.at[me_x]
            else:
                source_at = source.at[to, pl.ds(start, stop - start)]
                target_at = target.at[me_x, pl.ds(start, stop - start)]
            copies.append(
                pltpu.make_async_remote_copy(
                    src_ref=source_at,
                    dst_ref=target_at,
                    send_sem=sems_x.at[kind, 0, offset],
                    recv_sem=sems_x.at[kind, 1, offset],
                    device_id={"gx": to},
                    device_id_type=pl.DeviceIdType.MESH,
                )
            )
        for copy in copies:
            copy.start()
        return copies

    table = tzt_ref[...]
    copies_a = []
    for kind, (start, stop) in enumerate(chunks):
        size = stop - start
        div = jnp.concatenate(
            [
                jnp.swapaxes(div_ref[:, group * rows + start : group * rows + stop, :], 0, 1)
                for group in range(groups)
            ],
            axis=0,
        )
        along = dot_split(div.reshape(groups * size * block_x, length_z), table)
        along = along.reshape(groups, size, block_x, length_z)
        for target in range(count_x):
            send_a[target, start:stop] = jnp.concatenate(
                [
                    along[group, :, :, target * slab : (target + 1) * slab]
                    for group in range(groups)
                ],
                axis=-1,
            )
        copies_a.append(to_x(kind, send_a, recv_a, start, stop))
    copies_t = to_x(2, total_ref, totals)
    recv_a[me_x] = send_a[me_x]

    lane = lax.broadcasted_iota(jnp.int32, (full_x, lanes), 1)
    group_of = lane // slab
    decay = decay_ref[...]
    gain = gain_ref[...]
    zero = gain == 0.0

    def power(base, count):
        result = None
        while count:
            if count & 1:
                result = base if result is None else result * base
            count >>= 1
            if count:
                base = base * base
        return result

    def up(value):
        return pltpu.roll(value, slab, 1)

    def down(value):
        return pltpu.roll(value, lanes - slab, 1)

    decay_rows = power(decay, rows)
    decay_block = power(decay_rows, groups)
    decay_full = power(decay_block, count_y)

    for copies, (start, stop) in zip(copies_a, chunks):
        for copy in copies:
            copy.wait()
        gathered = jnp.concatenate(
            [
                jnp.concatenate([recv_a[place, row] for place in range(count_x)], axis=0)
                for row in range(start, stop)
            ],
            axis=1,
        )
        modes = dot_split(tx_ref[...], gathered)
        for row in range(start, stop):
            hat[row] = modes[:, (row - start) * lanes : (row - start + 1) * lanes]

    forward = hat[0]
    for row in range(1, rows):
        forward = decay * forward + hat[row]
    backward = hat[rows - 1]
    for row in range(rows - 2, -1, -1):
        backward = decay * backward + hat[row]
    forward_block = forward
    for group in range(1, groups):
        forward_block = jnp.where(
            group_of == group, forward + decay_rows * up(forward_block), forward_block
        )
    backward_block = backward
    for group in range(groups - 2, -1, -1):
        backward_block = jnp.where(
            group_of == group, backward + decay_rows * down(backward_block), backward_block
        )
    sums[me_y] = jnp.where(group_of == 0, backward_block, forward_block)
    copies_s = []
    for offset in range(1, count_y):
        copies_s.append(
            pltpu.make_async_remote_copy(
                src_ref=sums.at[me_y],
                dst_ref=sums.at[me_y],
                send_sem=sems_y.at[0, offset],
                recv_sem=sems_y.at[1, offset],
                device_id={"gy": lax.rem(me_y + offset, count_y)},
                device_id_type=pl.DeviceIdType.MESH,
            )
        )
    for copy in copies_s:
        copy.start()
    for copy in copies_s:
        copy.wait()

    from_low = jnp.zeros_like(decay)
    all_low = jnp.zeros_like(decay)
    power_low = jnp.ones_like(decay)
    from_high = jnp.zeros_like(decay)
    all_high = jnp.zeros_like(decay)
    power_high = jnp.ones_like(decay)
    for place in range(count_y):
        part = sums[place]
        all_low = all_low * decay_block + part
        from_low = jnp.where(place < me_y, from_low * decay_block + part, from_low)
        power_low = jnp.where(place < me_y, power_low * decay_block, power_low)
        other = count_y - 1 - place
        part = sums[other]
        all_high = all_high * decay_block + part
        from_high = jnp.where(other > me_y, from_high * decay_block + part, from_high)
        power_high = jnp.where(other > me_y, power_high * decay_block, power_high)
    first = group_of == 0

    def swap(value):
        return up(value) if groups == 2 else jnp.where(first, up(value), down(value))

    whole = jnp.where(first, all_high, all_low)
    image = jnp.where(
        zero,
        0.0,
        (whole + decay_full * swap(whole)) / jnp.where(zero, 1.0, 1.0 - decay_full * decay_full),
    )
    entering = jnp.where(first, from_high, from_low) + jnp.where(
        first, power_high, power_low
    ) * swap(image)
    carry_up = up(entering)
    for group in range(1, groups):
        carry_up = jnp.where(group_of == group, up(forward + decay_rows * carry_up), carry_up)
    carry_down = down(entering)
    for group in range(groups - 2, -1, -1):
        carry_down = jnp.where(
            group_of == group, down(backward + decay_rows * carry_down), carry_down
        )

    top = slice(0, 8)
    mean = jnp.where(first, whole, up(whole))
    for group in range(2, groups):
        mean = jnp.where(group_of == group, up(mean), mean)
    mean = mean[top] * (1.0 / (block_y * count_y))
    flat = jnp.zeros_like(mean)
    flats = [flat]
    position = (me_y * block_y + group_of[top] * rows).astype(jnp.float32)
    ahead = carry_up
    left = [ahead]
    for row in range(rows):
        ahead = decay * ahead + hat[row]
        left.append(ahead)
        flat = flat + (ahead[top] - (position + (row + 1.0)) * mean)
        flats.append(flat)
    offset_flat = jnp.zeros_like(mean)
    for group in range(1, groups):
        offset_flat = jnp.where(
            group_of[top] == group, up(offset_flat + flats[rows]), offset_flat
        )
    behind = carry_down
    pressures = [None] * (rows + 1)
    for row in range(rows, -1, -1):
        if row < rows:
            behind = decay * behind + hat[row]
        pressure = gain * (decay * left[row] + behind)
        special = jnp.where(zero[top], flats[row] + offset_flat, pressure[top])
        pressures[row] = jnp.concatenate([special, pressure[8:]], axis=0)
    back = dot_full(txt_ref[...], jnp.concatenate(pressures, axis=1))
    for target in range(count_x):
        for row in range(rows + 1):
            columns = slice(row * lanes, (row + 1) * lanes)
            send_b[target, row] = back[target * block_x : (target + 1) * block_x, columns]
            if target < count_x - 1:
                after = (target + 1) * block_x
                send_e[target, row : row + 1, :] = back[after : after + 1, columns]
        if target == count_x - 1:
            send_e[target] = jnp.zeros(send_e.shape[1:], jnp.float32)
    copies_e = to_x(3, send_e, recv_e)
    copies_high = to_x(4, send_b, recv_b, half, rows + 1)
    copies_low = to_x(5, send_b, recv_b, 0, half)
    recv_b[me_x] = send_b[me_x]
    recv_e[me_x] = send_e[me_x]
    for copy in copies_t:
        copy.wait()
    running = jnp.zeros_like(total_ref)
    for place in range(count_x - 1):
        running = jnp.where(place < me_x, running + totals[place], running)
    attenuation = extinction / full_x
    for at_x in range(block_x):
        column = smoke_ref[at_x]
        thickness = attenuation * column
        absorbed = jnp.tanh(0.5 * thickness) * (1.0 + jnp.exp(-thickness))
        emission_ref[at_x] = jnp.exp(-attenuation * running) * absorbed * (1.0 / attenuation)
        running = running + column

    table_back = tz_ref[...]
    for copy in copies_e:
        copy.wait()
    for group in range(groups):
        size = rows + (group == groups - 1)
        edge[group * rows : group * rows + size, :] = jnp.concatenate(
            [
                recv_e[place][:size, group * slab : (group + 1) * slab]
                for place in range(count_x)
            ],
            axis=-1,
        )
    following = dot_full(edge[...], table_back)[:block_y]
    after = None
    for copies, (start, stop) in ((copies_high, (half, rows + 1)), (copies_low, (0, half))):
        for copy in copies:
            copy.wait()
        size = stop - start
        field = jnp.concatenate(
            [
                jnp.concatenate(
                    [
                        recv_b[place, start:stop][..., group * slab : (group + 1) * slab]
                        for place in range(count_x)
                    ],
                    axis=-1,
                )
                for group in range(groups)
            ],
            axis=0,
        )
        field = dot_full(field.reshape(groups * size * block_x, length_z), table_back)
        field = field.reshape(groups, size, block_x, length_z)
        if after is not None:
            field = jnp.concatenate([field, after], axis=1)
        after = field[:, :1]
        for group in range(groups):
            at_y = group * rows + start
            middle = jnp.swapaxes(field[group, :half], 0, 1)
            ahead_x = jnp.concatenate([middle[1:], following[None, at_y : at_y + half]], axis=0)
            shape = middle.shape
            line = lax.broadcasted_iota(jnp.int32, shape, 1)
            ahead_y = jnp.where(
                line == half - 1, field[group, half][:, None, :], jnp.roll(middle, -1, axis=1)
            )
            ahead_z = pltpu.roll(middle, length_z - 1, 2)
            opened = (
                lax.broadcasted_iota(jnp.int32, shape, 0) + me_x * block_x < full_x - 1,
                line + (me_y * block_y + at_y) < block_y * count_y - 1,
                lax.broadcasted_iota(jnp.int32, shape, 2) < length_z - 1,
            )
            for axis_id, ahead in enumerate((ahead_x, ahead_y, ahead_z)):
                value = lifted_ref[axis_id, :, at_y : at_y + half, :] - (ahead - middle)
                out_ref[axis_id, :, at_y : at_y + half, :] = jnp.where(
                    opened[axis_id], value, 0.0
                )


def step_kernel(
    count_x,
    count_y,
    velocity_ref,
    density_ref,
    tz_ref,
    tzt_ref,
    tx_ref,
    txt_ref,
    decay_ref,
    gain_ref,
    out_ref,
    emission_ref,
    wide,
    middle,
    face_x,
    face_y,
    sent,
    received,
    lifted,
    smoke,
    div,
    total,
    *rest,
):
    me_x = lax.axis_index("gx")
    me_y = lax.axis_index("gy")
    *rest, fetched = rest
    given = (velocity_ref, density_ref, tz_ref, tzt_ref, tx_ref, txt_ref, decay_ref, gain_ref)
    held, rest = rest[-len(given) :], rest[: -len(given)]
    fetches = [
        pltpu.make_async_copy(source, target, fetched.at[index])
        for index, (source, target) in enumerate(zip(given, held))
    ]
    for fetch in fetches:
        fetch.start()
    barrier = pltpu.get_barrier_semaphore()

    def greet(to_x, to_y):
        pl.semaphore_signal(
            barrier,
            inc=1,
            device_id={"gx": to_x, "gy": to_y},
            device_id_type=pl.DeviceIdType.MESH,
        )

    for offset in range(1, count_x):
        greet(lax.rem(me_x + offset, count_x), me_y)
    for offset in range(1, count_y):
        greet(me_x, lax.rem(me_y + offset, count_y))
    for offset_x in (-1, 1):
        for offset_y in (-1, 1):
            to_x = me_x + offset_x
            to_y = me_y + offset_y

            @pl.when((to_x >= 0) & (to_x < count_x) & (to_y >= 0) & (to_y < count_y))
            def _():
                greet(to_x, to_y)

    def meet():
        beside_x = 2 - (me_x == 0).astype(jnp.int32) - (me_x == count_x - 1).astype(jnp.int32)
        beside_y = 2 - (me_y == 0).astype(jnp.int32) - (me_y == count_y - 1).astype(jnp.int32)
        pl.semaphore_wait(barrier, count_x + count_y - 2 + beside_x * beside_y)

    for fetch in fetches[:2]:
        fetch.wait()
    advect_part(
        count_x,
        count_y,
        meet,
        *held[:2],
        lifted,
        smoke,
        div,
        wide,
        middle,
        face_x,
        face_y,
        sent,
        received,
    )
    total[...] = jnp.sum(smoke[...], axis=0)
    for fetch in fetches[2:]:
        fetch.wait()
    solve_part(
        count_x,
        count_y,
        div,
        lifted,
        total,
        *held[2:],
        out_ref,
        emission_ref,
        smoke,
        *rest,
    )


def per_device(velocity, density):
    block_x, block_y, length_z = density.shape
    count_x = lax.axis_size("gx")
    count_y = lax.axis_size("gy")
    full_x = block_x * count_x
    slab = length_z // count_x
    lanes = 128
    groups = lanes // slab
    rows = block_y // groups
    padded = -(-(rows + 1) // 8) * 8
    table_z = cosine_table(length_z)
    table_x = cosine_table(full_x)
    decay, gain = mode_tables(full_x, length_z, slab, groups, lax.axis_index("gx") * slab)
    operands = (
        velocity,
        density,
        jnp.asarray(table_z),
        jnp.asarray(table_z.T.copy()),
        jnp.asarray(table_x),
        jnp.asarray(table_x.T.copy()),
        decay,
        gain,
    )
    vmem = pl.BlockSpec(memory_space=pltpu.VMEM)

    def buffer(*shape):
        return pltpu.VMEM(shape, jnp.float32)

    return pl.pallas_call(
        functools.partial(step_kernel, count_x, count_y),
        out_shape=(
            jax.ShapeDtypeStruct(velocity.shape, jnp.float32),
            jax.ShapeDtypeStruct(density.shape, jnp.float32),
        ),
        in_specs=[pl.BlockSpec(memory_space=pltpu.HBM)] * 8,
        out_specs=(vmem, vmem),
        scratch_shapes=[
            buffer(4, block_x + 4, block_y + 32, length_z),
            buffer(4, block_x + 5, block_y + 32, length_z),
            buffer(block_x + 1, block_y, length_z),
            buffer(block_x, block_y + 8, length_z),
            pltpu.SemaphoreType.DMA((17,)),
            pltpu.SemaphoreType.DMA((17,)),
            buffer(3, block_x, block_y, length_z),
            buffer(block_x, block_y, length_z),
            buffer(block_x, block_y, length_z),
            buffer(block_y, length_z),
            buffer(count_x, rows, block_x, lanes),
            buffer(count_x, rows, block_x, lanes),
            buffer(count_x, rows + 1, block_x, lanes),
            buffer(count_x, rows + 1, block_x, lanes),
            buffer(count_x, padded, lanes),
            buffer(count_x, padded, lanes),
            buffer(block_y + 8, length_z),
            buffer(count_x, block_y, length_z),
            buffer(count_y, full_x, lanes),
            buffer(rows, full_x, lanes),
            pltpu.SemaphoreType.DMA((6, 2, count_x)),
            pltpu.SemaphoreType.DMA((2, count_y)),
            *[pltpu.VMEM(value.shape, value.dtype) for value in operands],
            pltpu.SemaphoreType.DMA((len(operands),)),
        ],
        compiler_params=pltpu.CompilerParams(
            collective_id=0, has_side_effects=True, vmem_limit_bytes=64 * 1024 * 1024
        ),
    )(*operands)


def solution(mesh):
    in_specs = (P(None, "gx", "gy", None), P("gx", "gy", None))
    out_specs = (P(None, "gx", "gy", None), P("gx", "gy", None))
    return jax.shard_map(
        per_device, mesh=mesh, in_specs=in_specs, out_specs=out_specs, check_vma=False
    )
```
